256 devices in a mesh: shot: 8 (over x, core), rcv: 32 (over y, z).
Axes of the slice: x: 4, y: 4, z: 8, core: 2. Of those that a mesh axis runs over, the one named last changes fastest.
Arguments:
- response: bfloat16 [256, 128, 64], P('shot', 'rcv'), may hold values from -0.0625 to 0.0625
- traces: bfloat16 [128, 256, 512], P('shot', 'rcv'), may hold values from -6 to 6
Outputs:
- multiples: bfloat16 [256, 256, 512], P('shot', 'rcv')
The draws below stay inside these ranges and needn't reach their ends.
All inputs are finite; a program needn't handle non-finite values.
Results may differ from the reference program's by a relative error of at most 0.001.
Values may be sent and summed in bfloat16 or wider, within the bound.
No kernel may reach another device: no remote copies, remote signals or barrier semaphores. Data moves between devices by JAX's collectives and lax.ppermute only.
A program may use at most 256 MiB of HBM per device.

```python
import jax
import jax.numpy as jnp
from jax import lax

POSITIONS = 128
TAPS = 64
SAMPLES = 512
SHOTS = 256
RECEIVERS = 256


def block_scale(stream_key, dims, pieces, least, top_value):
    loudness = 1.0
    for dim, blocks in pieces:
        draws = jax.random.uniform(jax.random.fold_in(jax.random.fold_in(stream_key, 6), dim), (blocks,), jnp.float32, least / len(pieces), top_value / len(pieces))
        loudness = loudness * jnp.repeat(jnp.exp(draws), dims[dim] // blocks).reshape((-1,) + (1,) * (len(dims) - 1 - dim))
    return loudness


def centred(key, extent, scale, bound, cuts=(), kind=jnp.bfloat16):
    array = jax.random.normal(key, extent, jnp.float32) * scale
    if len(cuts) > 0:
        array = block_scale(key, extent, cuts, -0.22, 0.18) * array
    return jnp.clip(array, min=-bound, max=bound).astype(kind)


def setup_inputs(seed: int = 0) -> dict:
    key_list = jax.random.split(jax.random.key(seed), 3)
    return {
        "response": centred(key_list[0], (SHOTS, POSITIONS, TAPS), (POSITIONS * TAPS) ** -0.5, 0.0625, ((0, 8), (1, 32))),
        "traces": centred(key_list[1], (POSITIONS, RECEIVERS, SAMPLES), 1.0, 6.0, ((0, 8), (1, 32))),
    }


def reference(response, traces):
    padded = jnp.pad(traces, ((0, 0), (0, 0), (TAPS, 0)))
    flat_size = RECEIVERS * SAMPLES

    def add_tap(tap_index, running):
        lag = jnp.asarray(tap_index).astype(jnp.int32)
        shifted = lax.dynamic_slice_in_dim(padded, (TAPS - lag).astype(jnp.int32), SAMPLES, 2)
        column = lax.dynamic_slice_in_dim(response, lag, 1, 2)[:, :, 0]
        return running + jnp.dot(column, shifted.reshape(POSITIONS, flat_size), preferred_element_type=jnp.float32)

    running = lax.fori_loop(0, TAPS, add_tap, jnp.zeros((SHOTS, flat_size), jnp.float32))
    return running.reshape(SHOTS, RECEIVERS, SAMPLES).astype(jnp.bfloat16)
```

```python
import functools

import jax
import jax.numpy as jnp
from jax import lax
from jax.experimental import pallas as pl
from jax.experimental.pallas import tpu as pltpu
from jax.sharding import PartitionSpec as P

PHASES = 8
RING4 = (0, 1, -1, -2)
RING8 = (0, 1, -1, -2, 3, 2, 4, 5)


def spread(value, axis, partner):
    size = lax.axis_size(axis)
    return lax.ppermute(value, axis, [(i, partner(i)) for i in range(size)])


def sign(coordinate):
    return 1 - 2 * (coordinate % 2)


def gather_response(piece):
    def along_z(step):
        def partner(i):
            y, z = i // 8, i % 8
            return y * 8 + step(z) % 8

        return partner

    def along_y(step):
        def partner(i):
            y, z = i // 8, i % 8
            return (step(y) % 4) * 8 + z

        return partner

    held = piece[None]
    for step in (lambda z: z + sign(z), lambda z: z - sign(z), lambda z: z + 3 * sign(z)):
        held = jnp.concatenate([held, spread(held, "rcv", along_z(step))], axis=0)
    return [held] + [
        spread(held, "rcv", along_y(lambda y, offset=offset: y + offset)) for offset in (1, 3, 2)
    ]


def gather_traces(piece):
    def along_x(offset):
        return lambda i: ((i // 2 + offset) % 4) * 2 + i % 2

    mine = [piece] + [spread(piece, "shot", along_x(offset)) for offset in (1, 3, 2)]
    other = [spread(block, "shot", lambda i: i ^ 1) for block in mine]
    return mine + other


def kernel(slots, r0, r1, r2, r3, t0, t1, t2, t3, t4, t5, t6, t7, out, traces_pad, band, total):
    responses = (r0, r1, r2, r3)
    traces = (t0, t1, t2, t3, t4, t5, t6, t7)
    for slot in range(8):
        block = slots[slot]
        traces_pad[block, :64, :] = jnp.zeros((64, 128), jnp.bfloat16)
        traces_pad[block, 64:, :] = traces[slot][...]
    for y_slot in range(4):
        y_here = slots[8 + y_slot]
        for half in range(2):
            block = y_here * 2 + half
            rows = jnp.concatenate(
                [responses[y_slot][slots[12 + half * 4 + q]].astype(jnp.float32) for q in range(4)],
                axis=0,
            )
            wide = jnp.concatenate([rows, jnp.zeros((16, 384), jnp.float32)], axis=1)
            for shift in range(4):
                band[block, shift * 16 : shift * 16 + 16, :] = pltpu.roll(
                    wide, 128 + 32 * shift, 1
                ).astype(jnp.bfloat16)
    for pair in range(4):
        even_rows, odd_rows, sides = [], [], []
        for group in range(5):
            sides.append(
                jnp.concatenate(
                    [traces_pad[2 * pair + i, 64 - 16 * group : 576 - 16 * group, :] for i in range(2)],
                    axis=1,
                )
            )
            for rows, step in ((even_rows, 2 * group), (odd_rows, 2 * group + 1)):
                if step <= 8:
                    for i in range(2):
                        for late in range(2):
                            first = (2 * step - late + 1) * 128
                            rows.append(band[2 * pair + i, :, first : first + 256])
        even = jnp.dot(
            jnp.concatenate(sides, axis=1),
            jnp.concatenate(even_rows, axis=0),
            preferred_element_type=jnp.float32,
        )
        odd = jnp.dot(
            jnp.concatenate(sides[:4], axis=1),
            jnp.concatenate(odd_rows, axis=0),
            preferred_element_type=jnp.float32,
        )
        if pair == 0:
            total[:512, :] = even
            total[512:520, :] = jnp.zeros((8, 256), jnp.float32)
        else:
            total[:512, :] += even
        total[8:520, :] += odd
    out[...] = total[:512, :]


def shards(response, traces):
    shots_here, _, taps = response.shape
    rcv_here, samples = traces.shape[1:]
    blocks = samples // PHASES
    shot, rcv = lax.axis_index("shot"), lax.axis_index("rcv")
    x, core, y, z = shot // 2, shot % 2, rcv // 8, rcv % 8
    slots = []
    for other in (core, 1 - core):
        slots += [((x - offset) % 4) * 2 + other for offset in (0, 1, 3, 2)]
    slots += [(y - offset) % 4 for offset in (0, 1, 3, 2)]
    where_z = jnp.array([RING8.index(o) if o in RING8 else RING8.index(o - 8) for o in range(8)], jnp.int32)
    slots += [where_z[(sign(z) * (wanted - z)) % 8] for wanted in range(8)]
    slots = jnp.stack([jnp.asarray(s, jnp.int32) for s in slots])

    resp_piece = jnp.transpose(response, (1, 2, 0)).reshape(4, taps * shots_here)
    trace_piece = jnp.transpose(traces.reshape(16, rcv_here, blocks, PHASES), (2, 1, 3, 0)).reshape(
        blocks * rcv_here, PHASES * 16
    )
    responses = gather_response(resp_piece)
    pieces = gather_traces(trace_piece)
    vmem = pl.BlockSpec(memory_space=pltpu.VMEM)
    product = pl.pallas_call(
        kernel,
        out_shape=jax.ShapeDtypeStruct((512, 256), jnp.float32),
        in_specs=[pl.BlockSpec(memory_space=pltpu.SMEM)] + [vmem] * 12,
        out_specs=vmem,
        scratch_shapes=[
            pltpu.VMEM((8, 576, 128), jnp.bfloat16),
            pltpu.VMEM((8, 64, 19 * 128), jnp.bfloat16),
            pltpu.VMEM((520, 256), jnp.float32),
        ],
        compiler_params=pltpu.CompilerParams(vmem_limit_bytes=48 * 2**20),
    )(slots, *responses, *pieces)
    product = product.astype(jnp.bfloat16).reshape(blocks, rcv_here, PHASES, shots_here)
    return jnp.transpose(product, (3, 1, 0, 2)).reshape(shots_here, rcv_here, samples)


def solution(mesh):
    placed = (P("shot", "rcv", None), P("shot", "rcv", None))
    return jax.shard_map(
        shards, mesh=mesh, in_specs=placed, out_specs=P("shot", "rcv", None), check_vma=False
    )
```

```python
import jax
import jax.numpy as jnp
from jax import lax
from jax.experimental import pallas as pl
from jax.experimental.pallas import tpu as pltpu
from jax.sharding import PartitionSpec as P

RING4 = (0, 1, 3, 2)
RING8 = (0, 1, 7, 6, 3, 2, 4, 5)
VMEM = pl.BlockSpec(memory_space=pltpu.VMEM)
PARAMS = pltpu.CompilerParams(vmem_limit_bytes=40 * 2**20)


def spread(value, axis, partner):
    size = lax.axis_size(axis)
    return lax.ppermute(value, axis, [(i, partner(i)) for i in range(size)])


def sign(coordinate):
    return 1 - 2 * (coordinate % 2)


def prepare_traces(traces, out, rows, turned):
    for part in range(4):
        lanes = traces[:, :, part * 128 : part * 128 + 128]
        rows[part] = lanes.astype(jnp.float32).reshape(128, 128)
    for part in range(4):
        by_receiver = [rows[part, pl.ds(r, 16, stride=8), :] for r in range(8)]
        turned[part * 128 : part * 128 + 128, :] = jnp.concatenate(by_receiver, axis=0).T
    skewed = [pltpu.roll(turned[pl.ds(d, 64, stride=8), :], 16 * d, 1) for d in range(8)]
    lane_block = lax.broadcasted_iota(jnp.int32, (64, 128), 1) // 16
    for r in range(8):
        mixed = skewed[0]
        for d in range(1, 8):
            mixed = jnp.where(lane_block == (r + d) % 8, skewed[d], mixed)
        turned[pl.ds(r, 64, stride=8), :] = pltpu.roll(mixed, (128 - 16 * r) % 128, 1)
    out[...] = turned[...].astype(jnp.bfloat16)


def assemble(mine, other, out):
    shot = lax.axis_index("shot")
    x, core = shot // 2, shot % 2
    for blocks, side in ((mine, core), (other, 1 - core)):
        for slot in range(4):
            place = ((x + 4 - RING4[slot]) % 4) * 2 + side
            out[place, :64, :] = jnp.zeros((64, 128), jnp.bfloat16)
            out[place, 64:, :] = blocks[slot]


def position_of(offset):
    slot = jnp.int32(0)
    for index in range(1, 8):
        slot = jnp.where(offset == RING8[index], index, slot)
    return slot


def add_products(offsets, responses, padded, band, total):
    rcv = lax.axis_index("rcv")
    y, z = rcv // 8, rcv % 8
    slots = [position_of((sign(z) * (wanted - z) + 64) % 8) for wanted in range(8)]
    for response, offset in zip(responses, offsets, strict=True):
        for half in range(2):
            rows = jnp.concatenate(
                [response[slots[half * 4 + q]].astype(jnp.float32) for q in range(4)], axis=0
            )
            wide = jnp.concatenate([rows, jnp.zeros((16, 384), jnp.float32)], axis=1)
            for shift in range(4):
                band[half, shift * 16 : shift * 16 + 16, :] = pltpu.roll(
                    wide, 128 + 32 * shift, 1
                ).astype(jnp.bfloat16)
        place = ((y + 4 - offset) % 4) * 2
        even_rows, odd_rows, sides = [], [], []
        for group in range(5):
            sides += [
                padded[place + half, 64 - 16 * group : 576 - 16 * group, :] for half in range(2)
            ]
            for rows, step in ((even_rows, 2 * group), (odd_rows, 2 * group + 1)):
                if step <= 8:
                    for half in range(2):
                        for late in range(2):
                            first = (2 * step - late + 1) * 128
                            rows.append(band[half, :, first : first + 256])
        total[...] += jnp.dot(
            jnp.concatenate(sides, axis=1),
            jnp.concatenate(even_rows, axis=0),
            preferred_element_type=jnp.float32,
        )
        odd = jnp.dot(
            jnp.concatenate(sides[:8], axis=1),
            jnp.concatenate(odd_rows, axis=0),
            preferred_element_type=jnp.float32,
        )
        total[8:, :] += odd[:504, :]


def first_kernel(own, padded, total, band):
    total[...] = jnp.zeros_like(total)
    add_products((0,), (own,), padded, band, total)


def middle_kernel(before, after, padded, so_far, total, band):
    total[...] = so_far[...]
    add_products((1, 3), (before, after), padded, band, total)


def last_kernel(across, padded, so_far, out, band, total, placed):
    total[...] = so_far[...]
    add_products((2,), (across,), padded, band, total)
    turned = total[...].T
    skewed = [pltpu.roll(turned[u * 32 : u * 32 + 32, :], u, 1) for u in range(8)]
    lane = lax.broadcasted_iota(jnp.int32, (32, 512), 1)
    for r in range(8):
        mixed = skewed[0]
        for u in range(1, 8):
            mixed = jnp.where(lane % 8 == (r + u) % 8, skewed[u], mixed)
        mixed = pltpu.roll(mixed, (512 - r) % 512, 1)
        for part in range(4):
            placed[part, pl.ds(r, 32, stride=8), :] = mixed[:, part * 128 : part * 128 + 128]
    for part in range(4):
        out[:, :, part * 128 : part * 128 + 128] = placed[part].reshape(32, 8, 128).astype(jnp.bfloat16)


def call(body, shape, dtype, operands, scratch, flops=0):
    return pl.pallas_call(
        body,
        out_shape=jax.ShapeDtypeStruct(shape, dtype),
        in_specs=[VMEM] * len(operands),
        out_specs=VMEM,
        scratch_shapes=[pltpu.VMEM(s, d) for s, d in scratch],
        compiler_params=PARAMS,
        cost_estimate=pl.CostEstimate(flops=flops, bytes_accessed=2**20, transcendentals=0),
    )(*operands)


def shards(response, traces):
    f32, bf16 = jnp.float32, jnp.bfloat16
    band = ((2, 64, 19 * 128), bf16)

    def along_z(step):
        return lambda i: (i // 8) * 8 + step(i % 8) % 8

    def along_y(offset):
        return lambda i: (i // 8 + offset) % 4 * 8 + i % 8

    def along_x(offset):
        return lambda i: ((i // 2 + offset) % 4) * 2 + i % 2

    held = jnp.transpose(response, (1, 2, 0)).reshape(1, 4, 2048)
    piece = call(prepare_traces, (512, 128), bf16, (traces,), [((4, 128, 128), f32), ((512, 128), f32)])
    for step in (lambda z: z + sign(z), lambda z: z - sign(z), lambda z: z + 3 * sign(z)):
        held = jnp.concatenate([held, spread(held, "rcv", along_z(step))], axis=0)
    before, after, across = [spread(held, "rcv", along_y(offset)) for offset in (1, 3, 2)]

    mine = jnp.stack([piece] + [spread(piece, "shot", along_x(offset)) for offset in (1, 3, 2)])
    other = spread(mine, "shot", lambda i: i ^ 1)
    padded = call(assemble, (8, 576, 128), bf16, (mine, other), [])
    work = 2 * 512 * 256 * 9 * 256
    total = call(first_kernel, (512, 256), f32, (held, padded), [band], work)
    total = call(middle_kernel, (512, 256), f32, (before, after, padded, total), [band], 2 * work)
    return call(
        last_kernel,
        (32, 8, 512),
        bf16,
        (across, padded, total),
        [band, ((512, 256), f32), ((4, 256, 128), f32)],
        work,
    )


def solution(mesh):
    placed = (P("shot", "rcv", None), P("shot", "rcv", None))
    return jax.shard_map(
        shards, mesh=mesh, in_specs=placed, out_specs=P("shot", "rcv", None), check_vma=False
    )
```

```python
import jax
import jax.numpy as jnp
from jax import lax
from jax.experimental import pallas as pl
from jax.experimental.pallas import tpu as pltpu
from jax.sharding import PartitionSpec as P

RING4 = (0, 1, 3, 2)
RING8 = (0, 1, 7, 6, 2, 3, 5, 4)
VMEM = pl.BlockSpec(memory_space=pltpu.VMEM)
PARAMS = pltpu.CompilerParams(vmem_limit_bytes=40 * 2**20)


def spread(value, axis, partner):
    size = lax.axis_size(axis)
    return lax.ppermute(value, axis, [(i, partner(i)) for i in range(size)])


def sign(coordinate):
    return 1 - 2 * (coordinate % 2)


def prepare_traces(traces, _, out, rows, turned):
    for part in range(4):
        lanes = traces[:, :, part * 128 : part * 128 + 128]
        rows[part] = lanes.astype(jnp.float32).reshape(128, 128)
    for part in range(4):
        by_receiver = [rows[part, pl.ds(r, 16, stride=8), :] for r in range(8)]
        turned[part * 128 : part * 128 + 128, :] = jnp.concatenate(by_receiver, axis=0).T
    skewed = [pltpu.roll(turned[pl.ds(d, 64, stride=8), :], 16 * d, 1) for d in range(8)]
    lane_block = lax.broadcasted_iota(jnp.int32, (64, 128), 1) // 16
    for r in range(8):
        mixed = skewed[0]
        for d in range(1, 8):
            mixed = jnp.where(lane_block == (r + d) % 8, skewed[d], mixed)
        turned[pl.ds(r, 64, stride=8), :] = pltpu.roll(mixed, (128 - 16 * r) % 128, 1)
    out[...] = turned[...].astype(jnp.bfloat16)


def assemble(mine, other, out):
    shot = lax.axis_index("shot")
    x, core = shot // 2, shot % 2
    for blocks, side in ((mine, core), (other, 1 - core)):
        for slot in range(4):
            place = ((x + 4 - RING4[slot]) % 4) * 2 + side
            out[place, :64, :] = jnp.zeros((64, 128), jnp.bfloat16)
            out[place, 64:, :] = blocks[slot]


def position_of(offset):
    slot = jnp.int32(0)
    for index in range(1, 8):
        slot = jnp.where(offset == RING8[index], index, slot)
    return slot


def add_products(offsets, responses, padded, band, total):
    rcv = lax.axis_index("rcv")
    y, z = rcv // 8, rcv % 8
    slots = [position_of((sign(z) * (wanted - z) + 64) % 8) for wanted in range(8)]
    for response, offset in zip(responses, offsets, strict=True):
        for half in range(2):
            rows = jnp.concatenate(
                [response[slots[half * 4 + q]].astype(jnp.float32) for q in range(4)], axis=0
            )
            wide = jnp.concatenate([rows, jnp.zeros((16, 384), jnp.float32)], axis=1)
            for shift in range(4):
                band[half, shift * 16 : shift * 16 + 16, :] = pltpu.roll(
                    wide, 128 + 32 * shift, 1
                ).astype(jnp.bfloat16)
        place = ((y + 4 - offset) % 4) * 2
        even_rows, odd_rows, sides = [], [], []
        for group in range(5):
            sides += [
                padded[place + half, 64 - 16 * group : 576 - 16 * group, :] for half in range(2)
            ]
            for rows, step in ((even_rows, 2 * group), (odd_rows, 2 * group + 1)):
                if step <= 8:
                    for half in range(2):
                        for late in range(2):
                            first = (2 * step - late + 1) * 128
                            rows.append(band[half, :, first : first + 256])
        total[...] += jnp.dot(
            jnp.concatenate(sides, axis=1),
            jnp.concatenate(even_rows, axis=0),
            preferred_element_type=jnp.float32,
        )
        odd = jnp.dot(
            jnp.concatenate(sides[:8], axis=1),
            jnp.concatenate(odd_rows, axis=0),
            preferred_element_type=jnp.float32,
        )
        total[8:, :] += odd[:504, :]


def first_kernel(own, padded, total, band):
    total[...] = jnp.zeros_like(total)
    add_products((0,), (own,), padded, band, total)


def middle_kernel(before, after, padded, so_far, total, band):
    total[...] = so_far[...]
    add_products((1, 3), (before, after), padded, band, total)


def last_kernel(across, padded, so_far, out, band, total, placed):
    total[...] = so_far[...]
    add_products((2,), (across,), padded, band, total)
    turned = total[...].T
    skewed = [pltpu.roll(turned[u * 32 : u * 32 + 32, :], u, 1) for u in range(8)]
    lane = lax.broadcasted_iota(jnp.int32, (32, 512), 1)
    for r in range(8):
        mixed = skewed[0]
        for u in range(1, 8):
            mixed = jnp.where(lane % 8 == (r + u) % 8, skewed[u], mixed)
        mixed = pltpu.roll(mixed, (512 - r) % 512, 1)
        for part in range(4):
            placed[part, pl.ds(r, 32, stride=8), :] = mixed[:, part * 128 : part * 128 + 128]
    for part in range(4):
        out[:, :, part * 128 : part * 128 + 128] = placed[part].reshape(32, 8, 128).astype(jnp.bfloat16)


def call(body, shape, dtype, operands, scratch, flops=0):
    return pl.pallas_call(
        body,
        out_shape=jax.ShapeDtypeStruct(shape, dtype),
        in_specs=[VMEM] * len(operands),
        out_specs=VMEM,
        scratch_shapes=[pltpu.VMEM(s, d) for s, d in scratch],
        compiler_params=PARAMS,
        cost_estimate=pl.CostEstimate(flops=flops, bytes_accessed=2**20, transcendentals=0),
    )(*operands)


def shards(response, traces):
    f32, bf16 = jnp.float32, jnp.bfloat16
    band = ((2, 64, 19 * 128), bf16)

    def along_z(step):
        return lambda i: (i // 8) * 8 + step(i % 8) % 8

    def along_y(offset):
        return lambda i: (i // 8 + offset) % 4 * 8 + i % 8

    def along_x(offset):
        return lambda i: ((i // 2 + offset) % 4) * 2 + i % 2

    held = jnp.transpose(response, (1, 2, 0)).reshape(1, 4, 2048)
    piece = call(prepare_traces, (512, 128), bf16, (traces, held), [((4, 128, 128), f32), ((512, 128), f32)])
    held = jnp.concatenate([held, spread(held, "rcv", along_z(lambda z: z + sign(z)))], axis=0)
    steps = [lambda z: z - sign(z), lambda z: z - 2 * sign(z), lambda z: z - 3 * sign(z)]
    held = jnp.concatenate([held] + [spread(held, "rcv", along_z(step)) for step in steps], axis=0)
    before, after, across = [spread(held, "rcv", along_y(offset)) for offset in (1, 3, 2)]

    mine = jnp.stack([piece] + [spread(piece, "shot", along_x(offset)) for offset in (1, 3, 2)])
    other = spread(mine, "shot", lambda i: i ^ 1)
    padded = call(assemble, (8, 576, 128), bf16, (mine, other), [])
    work = 2 * 512 * 256 * 9 * 256
    total = call(first_kernel, (512, 256), f32, (held, padded), [band], work)
    total = call(middle_kernel, (512, 256), f32, (before, after, padded, total), [band], 2 * work)
    return call(
        last_kernel,
        (32, 8, 512),
        bf16,
        (across, padded, total),
        [band, ((512, 256), f32), ((4, 256, 128), f32)],
        work,
    )


def solution(mesh):
    placed = (P("shot", "rcv", None), P("shot", "rcv", None))
    return jax.shard_map(
        shards, mesh=mesh, in_specs=placed, out_specs=P("shot", "rcv", None), check_vma=False
    )
```

```python
import jax
import jax.numpy as jnp
from jax import lax
from jax.experimental import pallas as pl
from jax.experimental.pallas import tpu as pltpu
from jax.sharding import PartitionSpec as P

RING4 = (0, 1, 3, 2)
RING8 = (0, 1, 2, 3, 7, 6, 5, 4)
VMEM = pl.BlockSpec(memory_space=pltpu.VMEM)
JOIN_COST = 2**33
PARAMS = pltpu.CompilerParams(vmem_limit_bytes=40 * 2**20)


def spread(value, axis, partner):
    size = lax.axis_size(axis)
    return lax.ppermute(value, axis, [(i, partner(i)) for i in range(size)])


def sign(coordinate):
    return 1 - 2 * (coordinate % 2)


def prepare_response(response, out, rows, turned):
    wide = response[...].astype(jnp.float32)
    rows[...] = jnp.concatenate([wide, jnp.zeros((128, 64), jnp.float32)], axis=1)
    by_position = jnp.concatenate([rows[pl.ds(k, 32, stride=4), :] for k in range(4)], axis=0)
    turned[...] = by_position.T[:64, :]
    skewed = [pltpu.roll(turned[pl.ds(u, 16, stride=4), :], 32 * u, 1) for u in range(4)]
    lane_block = lax.broadcasted_iota(jnp.int32, (16, 128), 1) // 32
    for k in range(4):
        mixed = skewed[0]
        for u in range(1, 4):
            mixed = jnp.where(lane_block == (k + u) % 4, skewed[u], mixed)
        out[k * 16 : k * 16 + 16, :] = pltpu.roll(mixed, (128 - 32 * k) % 128, 1).astype(jnp.bfloat16)


def prepare_traces(traces, _, out, rows, turned):
    for part in range(4):
        lanes = traces[:, :, part * 128 : part * 128 + 128]
        rows[part] = lanes.astype(jnp.float32).reshape(128, 128)
    for part in range(4):
        by_receiver = [rows[part, pl.ds(r, 16, stride=8), :] for r in range(8)]
        turned[part * 128 : part * 128 + 128, :] = jnp.concatenate(by_receiver, axis=0).T
    skewed = [pltpu.roll(turned[pl.ds(d, 64, stride=8), :], 16 * d, 1) for d in range(8)]
    lane_block = lax.broadcasted_iota(jnp.int32, (64, 128), 1) // 16
    for r in range(8):
        mixed = skewed[0]
        for d in range(1, 8):
            mixed = jnp.where(lane_block == (r + d) % 8, skewed[d], mixed)
        turned[pl.ds(r, 64, stride=8), :] = pltpu.roll(mixed, (128 - 16 * r) % 128, 1)
    out[...] = turned[...].astype(jnp.bfloat16)


def assemble(own, after, before, across, others, other_across, out):
    shot = lax.axis_index("shot")
    x, core = shot // 2, shot % 2
    mine = (own, after, before, across)
    theirs = (others.at[0], others.at[1], others.at[2], other_across)
    for blocks, side in ((mine, core), (theirs, 1 - core)):
        for slot in range(4):
            place = ((x + 4 - RING4[slot]) % 4) * 2 + side
            out[place, :64, :] = jnp.zeros((64, 128), jnp.bfloat16)
            out[place, 64:, :] = blocks[slot][...]


def join(first, second, out):
    count = first.shape[0]
    out[:count] = first[...]
    out[count:] = second[...]


def position_of(offset):
    slot = jnp.int32(0)
    for index in range(1, 8):
        slot = jnp.where(offset == RING8[index], index, slot)
    return slot


def add_products(offsets, responses, padded, band, rows_f32, total):
    rcv = lax.axis_index("rcv")
    y, z = rcv // 8, rcv % 8
    slots = [position_of((sign(z) * (wanted - z) + 64) % 8) for wanted in range(8)]
    for response, offset in zip(responses, offsets, strict=True):
        for half in range(2):
            for q in range(4):
                piece = response[slots[half * 4 + q]]
                rows_f32[half, q * 64 : q * 64 + 64, :] = piece.astype(jnp.float32)
            wide = jnp.concatenate(
                [rows_f32[half, pl.ds(m, 16, stride=16), :] for m in range(16)]
                + [jnp.zeros((16, 384), jnp.float32)],
                axis=1,
            )
            for shift in range(4):
                band[half, shift * 16 : shift * 16 + 16, :] = pltpu.roll(
                    wide, 128 + 32 * shift, 1
                ).astype(jnp.bfloat16)
        place = ((y + 4 - offset) % 4) * 2
        even_rows, odd_rows, sides = [], [], []
        for group in range(5):
            sides += [
                padded[place + half, 64 - 16 * group : 576 - 16 * group, :] for half in range(2)
            ]
            for rows, step in ((even_rows, 2 * group), (odd_rows, 2 * group + 1)):
                if step <= 8:
                    for half in range(2):
                        for late in range(2):
                            first = (2 * step - late + 1) * 128
                            rows.append(band[half, :, first : first + 256])
        total[...] += jnp.dot(
            jnp.concatenate(sides, axis=1),
            jnp.concatenate(even_rows, axis=0),
            preferred_element_type=jnp.float32,
        )
        odd = jnp.dot(
            jnp.concatenate(sides[:8], axis=1),
            jnp.concatenate(odd_rows, axis=0),
            preferred_element_type=jnp.float32,
        )
        total[8:, :] += odd[:504, :]


def first_kernel(own, padded, total, band, rows):
    total[...] = jnp.zeros_like(total)
    add_products((0,), (own,), padded, band, rows, total)


def middle_kernel(before, after, padded, so_far, total, band, rows):
    total[...] = so_far[...]
    add_products((1, 3), (before, after), padded, band, rows, total)


def last_kernel(across, padded, so_far, out, band, rows, total, placed):
    total[...] = so_far[...]
    add_products((2,), (across,), padded, band, rows, total)
    turned = total[...].T
    skewed = [pltpu.roll(turned[u * 32 : u * 32 + 32, :], u, 1) for u in range(8)]
    lane = lax.broadcasted_iota(jnp.int32, (32, 512), 1)
    for r in range(8):
        mixed = skewed[0]
        for u in range(1, 8):
            mixed = jnp.where(lane % 8 == (r + u) % 8, skewed[u], mixed)
        mixed = pltpu.roll(mixed, (512 - r) % 512, 1)
        for part in range(4):
            placed[part, pl.ds(r, 32, stride=8), :] = mixed[:, part * 128 : part * 128 + 128]
    for part in range(4):
        out[:, :, part * 128 : part * 128 + 128] = placed[part].reshape(32, 8, 128).astype(jnp.bfloat16)


def call(body, shape, dtype, operands, scratch, flops=0):
    return pl.pallas_call(
        body,
        out_shape=jax.ShapeDtypeStruct(shape, dtype),
        in_specs=[VMEM] * len(operands),
        out_specs=VMEM,
        scratch_shapes=[pltpu.VMEM(s, d) for s, d in scratch],
        compiler_params=PARAMS,
        cost_estimate=pl.CostEstimate(flops=flops, bytes_accessed=2**20, transcendentals=0),
    )(*operands)


def shards(response, traces):
    f32, bf16 = jnp.float32, jnp.bfloat16
    band = [((2, 64, 19 * 128), bf16), ((2, 256, 128), f32)]

    def along_z(step):
        return lambda i: (i // 8) * 8 + step(i % 8) % 8

    def along_y(offset):
        return lambda i: (i // 8 + offset) % 4 * 8 + i % 8

    def along_x(offset):
        return lambda i: ((i // 2 + offset) % 4) * 2 + i % 2

    def swap(value):
        return spread(value, "shot", lambda i: i ^ 1)

    held = call(
        prepare_response,
        (64, 128),
        bf16,
        (response.reshape(128, 64),),
        [((128, 128), f32), ((64, 128), f32)],
    )
    held = held[None]
    piece = call(prepare_traces, (512, 128), bf16, (traces, held), [((4, 128, 128), f32), ((512, 128), f32)])
    for step in (lambda z: z + sign(z), lambda z: z - 2 * sign(z), lambda z: z - sign(z)):
        arrived = spread(held, "rcv", along_z(step))
        held = call(join, (2 * held.shape[0], 64, 128), bf16, (held, arrived), [], JOIN_COST)
    before, after, across = [spread(held, "rcv", along_y(offset)) for offset in (1, 3, 2)]

    next_piece = spread(piece, "shot", along_x(1))
    previous_piece = spread(piece, "shot", along_x(3))
    far_piece = spread(next_piece, "shot", along_x(1))
    others = swap(jnp.stack([piece, next_piece, previous_piece]))
    pieces = (piece, next_piece, previous_piece, far_piece, others, swap(far_piece))
    padded = call(assemble, (8, 576, 128), bf16, pieces, [])
    work = 2 * 512 * 256 * 9 * 256
    total = call(first_kernel, (512, 256), f32, (held, padded), band, work)
    total = call(middle_kernel, (512, 256), f32, (before, after, padded, total), band, 2 * work)
    return call(
        last_kernel,
        (32, 8, 512),
        bf16,
        (across, padded, total),
        band + [((512, 256), f32), ((4, 256, 128), f32)],
        work,
    )


def solution(mesh):
    placed = (P("shot", "rcv", None), P("shot", "rcv", None))
    return jax.shard_map(
        shards, mesh=mesh, in_specs=placed, out_specs=P("shot", "rcv", None), check_vma=False
    )
```

```python
import functools

import jax
import jax.numpy as jnp
from jax import lax
from jax.experimental import pallas as pl
from jax.experimental.pallas import tpu as pltpu
from jax.sharding import PartitionSpec as P

RING8 = (0, 1, 2, 3, 7, 6, 5, 4)
VMEM = pl.BlockSpec(memory_space=pltpu.VMEM)
JOIN_COST = 2**33
PARAMS = pltpu.CompilerParams(vmem_limit_bytes=40 * 2**20)


def spread(value, axis, partner):
    size = lax.axis_size(axis)
    return lax.ppermute(value, axis, [(i, partner(i)) for i in range(size)])


def sign(coordinate):
    return 1 - 2 * (coordinate % 2)


def prepare_response(response, out, rows, turned):
    wide = response[...].astype(jnp.float32)
    rows[...] = jnp.concatenate([wide, jnp.zeros((128, 64), jnp.float32)], axis=1)
    by_position = jnp.concatenate([rows[pl.ds(k, 32, stride=4), :] for k in range(4)], axis=0)
    turned[...] = by_position.T[:64, :]
    skewed = [pltpu.roll(turned[pl.ds(u, 16, stride=4), :], 32 * u, 1) for u in range(4)]
    lane_block = lax.broadcasted_iota(jnp.int32, (16, 128), 1) // 32
    for k in range(4):
        mixed = skewed[0]
        for u in range(1, 4):
            mixed = jnp.where(lane_block == (k + u) % 4, skewed[u], mixed)
        out[k * 16 : k * 16 + 16, :] = pltpu.roll(mixed, (128 - 32 * k) % 128, 1).astype(jnp.bfloat16)


def prepare_traces(own, other, _, out, rows, turned):
    lane_block = lax.broadcasted_iota(jnp.int32, (64, 128), 1) // 16
    for side, traces in enumerate((own, other)):
        for part in range(4):
            lanes = traces[:, :, part * 128 : part * 128 + 128]
            rows[side, part] = lanes.astype(jnp.float32).reshape(128, 128)
        for part in range(4):
            by_receiver = [rows[side, part, pl.ds(r, 16, stride=8), :] for r in range(8)]
            turned[side, part * 128 : part * 128 + 128, :] = jnp.concatenate(by_receiver, axis=0).T
        skewed = [pltpu.roll(turned[side, pl.ds(d, 64, stride=8), :], 16 * d, 1) for d in range(8)]
        for r in range(8):
            mixed = skewed[0]
            for d in range(1, 8):
                mixed = jnp.where(lane_block == (r + d) % 8, skewed[d], mixed)
            turned[side, pl.ds(r, 64, stride=8), :] = pltpu.roll(mixed, (128 - 16 * r) % 128, 1)
        out[side] = turned[side].astype(jnp.bfloat16)


def assemble(own, near, near_swapped, far, far_swapped, out):
    shot = lax.axis_index("shot")
    x, core = shot // 2, shot % 2
    back = 4 - sign(core)
    blocks = (
        (own.at[0], x, core),
        (own.at[1], x, 1 - core),
        (near.at[0], x + back, core),
        (near.at[1], x + back, 1 - core),
        (near_swapped.at[0], x + 8 - back, 1 - core),
        (near_swapped.at[1], x + 8 - back, core),
        (far, x + 2, core),
        (far_swapped, x + 2, 1 - core),
    )
    for block, chip, side in blocks:
        place = (chip % 4) * 2 + side
        out[place, :64, :] = jnp.zeros((64, 128), jnp.bfloat16)
        out[place, 64:, :] = block[...]


def join(first, second, out):
    count = first.shape[0]
    out[:count] = first[...]
    out[count:] = second[...]


def position_of(offset):
    slot = jnp.int32(0)
    for index in range(1, 8):
        slot = jnp.where(offset == RING8[index], index, slot)
    return slot


def add_products(offsets, responses, padded, band, rows_f32, total):
    rcv = lax.axis_index("rcv")
    y, z = rcv // 8, rcv % 8
    slots = [position_of((sign(z) * (wanted - z) + 64) % 8) for wanted in range(8)]
    for response, offset in zip(responses, offsets, strict=True):
        for half in range(2):
            for q in range(4):
                piece = response[slots[half * 4 + q]]
                rows_f32[half, q * 64 : q * 64 + 64, :] = piece.astype(jnp.float32)
            wide = jnp.concatenate(
                [rows_f32[half, pl.ds(m, 16, stride=16), :] for m in range(16)]
                + [jnp.zeros((16, 384), jnp.float32)],
                axis=1,
            )
            for shift in range(4):
                band[half, shift * 16 : shift * 16 + 16, :] = pltpu.roll(
                    wide, 128 + 32 * shift, 1
                ).astype(jnp.bfloat16)
        place = ((y + 4 - offset) % 4) * 2
        even_rows, odd_rows, sides = [], [], []
        for group in range(5):
            sides += [
                padded[place + half, 64 - 16 * group : 576 - 16 * group, :] for half in range(2)
            ]
            for rows, step in ((even_rows, 2 * group), (odd_rows, 2 * group + 1)):
                if step <= 8:
                    for half in range(2):
                        for late in range(2):
                            first = (2 * step - late + 1) * 128
                            rows.append(band[half, :, first : first + 256])
        total[...] += jnp.dot(
            jnp.concatenate(sides, axis=1),
            jnp.concatenate(even_rows, axis=0),
            preferred_element_type=jnp.float32,
        )
        odd = jnp.dot(
            jnp.concatenate(sides[:8], axis=1),
            jnp.concatenate(odd_rows, axis=0),
            preferred_element_type=jnp.float32,
        )
        total[8:, :] += odd[:504, :]


def first_kernel(own, padded, total, band, rows):
    total[...] = jnp.zeros_like(total)
    add_products((0,), (own,), padded, band, rows, total)


def middle_kernel(offset, response, padded, so_far, total, band, rows):
    total[...] = so_far[...]
    add_products((offset,), (response,), padded, band, rows, total)


def last_kernel(across, padded, so_far, out, band, rows, total, placed):
    total[...] = so_far[...]
    add_products((2,), (across,), padded, band, rows, total)
    turned = total[...].T
    skewed = [pltpu.roll(turned[u * 32 : u * 32 + 32, :], u, 1) for u in range(8)]
    lane = lax.broadcasted_iota(jnp.int32, (32, 512), 1)
    for r in range(8):
        mixed = skewed[0]
        for u in range(1, 8):
            mixed = jnp.where(lane % 8 == (r + u) % 8, skewed[u], mixed)
        mixed = pltpu.roll(mixed, (512 - r) % 512, 1)
        for part in range(4):
            placed[part, pl.ds(r, 32, stride=8), :] = mixed[:, part * 128 : part * 128 + 128]
    for part in range(4):
        out[:, :, part * 128 : part * 128 + 128] = placed[part].reshape(32, 8, 128).astype(jnp.bfloat16)


def call(body, shape, dtype, operands, scratch, flops=0):
    return pl.pallas_call(
        body,
        out_shape=jax.ShapeDtypeStruct(shape, dtype),
        in_specs=[VMEM] * len(operands),
        out_specs=VMEM,
        scratch_shapes=[pltpu.VMEM(s, d) for s, d in scratch],
        compiler_params=PARAMS,
        cost_estimate=pl.CostEstimate(flops=flops, bytes_accessed=2**20, transcendentals=0),
    )(*operands)


def shards(response, traces):
    f32, bf16 = jnp.float32, jnp.bfloat16
    band = [((2, 64, 19 * 128), bf16), ((2, 256, 128), f32)]

    def along_z(step):
        return lambda i: (i // 8) * 8 + step(i % 8) % 8

    def along_y(offset):
        return lambda i: (i // 8 + offset) % 4 * 8 + i % 8

    def along_x(i):
        return ((i // 2 + sign(i)) % 4) * 2 + i % 2

    def swap(value):
        return spread(value, "shot", lambda i: i ^ 1)

    held = call(
        prepare_response,
        (64, 128),
        bf16,
        (response.reshape(128, 64),),
        [((128, 128), f32), ((64, 128), f32)],
    )
    held = held[None]
    both = call(
        prepare_traces,
        (2, 512, 128),
        bf16,
        (traces, swap(traces), held),
        [((2, 4, 128, 128), f32), ((2, 512, 128), f32)],
    )
    for step in (lambda z: z + sign(z), lambda z: z - 2 * sign(z), lambda z: z - sign(z)):
        arrived = spread(held, "rcv", along_z(step))
        held = call(join, (2 * held.shape[0], 64, 128), bf16, (held, arrived), [], JOIN_COST)
    before, after, across = [spread(held, "rcv", along_y(offset)) for offset in (1, 3, 2)]

    near = spread(both, "shot", along_x)
    far = spread(near[0], "shot", along_x)
    pieces = (both, near, swap(near), far, swap(far))
    padded = call(assemble, (8, 576, 128), bf16, pieces, [])
    work = 2 * 512 * 256 * 9 * 256
    total = call(first_kernel, (512, 256), f32, (held, padded), band, work)
    for offset, block in ((3, after), (1, before)):
        body = functools.partial(middle_kernel, offset)
        total = call(body, (512, 256), f32, (block, padded, total), band, work)
    return call(
        last_kernel,
        (32, 8, 512),
        bf16,
        (across, padded, total),
        band + [((512, 256), f32), ((4, 256, 128), f32)],
        work,
    )


def solution(mesh):
    placed = (P("shot", "rcv", None), P("shot", "rcv", None))
    return jax.shard_map(
        shards, mesh=mesh, in_specs=placed, out_specs=P("shot", "rcv", None), check_vma=False
    )
```

```python
import functools

import jax
import jax.numpy as jnp
from jax import lax
from jax.experimental import pallas as pl
from jax.experimental.pallas import tpu as pltpu
from jax.sharding import PartitionSpec as P

RING8 = (0, 1, 5, 4, 2, 3, 7, 6)
VMEM = pl.BlockSpec(memory_space=pltpu.VMEM)
JOIN_COST = 2**33
PARAMS = pltpu.CompilerParams(vmem_limit_bytes=40 * 2**20)


def spread(value, axis, partner):
    size = lax.axis_size(axis)
    return lax.ppermute(value, axis, [(i, partner(i)) for i in range(size)])


def sign(coordinate):
    return 1 - 2 * (coordinate % 2)


def prepare_response(response, out, rows, turned):
    wide = response[...].astype(jnp.float32)
    rows[...] = jnp.concatenate([wide, jnp.zeros((128, 64), jnp.float32)], axis=1)
    by_position = jnp.concatenate([rows[pl.ds(k, 32, stride=4), :] for k in range(4)], axis=0)
    turned[...] = by_position.T[:64, :]
    skewed = [pltpu.roll(turned[pl.ds(u, 16, stride=4), :], 32 * u, 1) for u in range(4)]
    lane_block = lax.broadcasted_iota(jnp.int32, (16, 128), 1) // 32
    for k in range(4):
        mixed = skewed[0]
        for u in range(1, 4):
            mixed = jnp.where(lane_block == (k + u) % 4, skewed[u], mixed)
        out[k * 16 : k * 16 + 16, :] = pltpu.roll(mixed, (128 - 32 * k) % 128, 1).astype(jnp.bfloat16)


def prepare_traces(own, other, _, out, rows, turned):
    lane_block = lax.broadcasted_iota(jnp.int32, (64, 128), 1) // 16
    for side, traces in enumerate((own, other)):
        for part in range(4):
            lanes = traces[:, :, part * 128 : part * 128 + 128]
            rows[side, part] = lanes.astype(jnp.float32).reshape(128, 128)
        for part in range(4):
            by_receiver = [rows[side, part, pl.ds(r, 16, stride=8), :] for r in range(8)]
            turned[side, part * 128 : part * 128 + 128, :] = jnp.concatenate(by_receiver, axis=0).T
        skewed = [pltpu.roll(turned[side, pl.ds(d, 64, stride=8), :], 16 * d, 1) for d in range(8)]
        for r in range(8):
            mixed = skewed[0]
            for d in range(1, 8):
                mixed = jnp.where(lane_block == (r + d) % 8, skewed[d], mixed)
            turned[side, pl.ds(r, 64, stride=8), :] = pltpu.roll(mixed, (128 - 16 * r) % 128, 1)
        out[side] = turned[side].astype(jnp.bfloat16)


def assemble(own, near, near_swapped, far, far_swapped, out):
    shot = lax.axis_index("shot")
    x, core = shot // 2, shot % 2
    back = 4 - sign(core)
    blocks = (
        (own.at[0], x, core),
        (own.at[1], x, 1 - core),
        (near.at[0], x + back, core),
        (near.at[1], x + back, 1 - core),
        (near_swapped.at[0], x + 8 - back, 1 - core),
        (near_swapped.at[1], x + 8 - back, core),
        (far, x + 2, core),
        (far_swapped, x + 2, 1 - core),
    )
    for block, chip, side in blocks:
        place = (chip % 4) * 2 + side
        out[place, :64, :] = jnp.zeros((64, 128), jnp.bfloat16)
        out[place, 64:, :] = block[...]


def join(*blocks):
    out = blocks[-1]
    count = blocks[0].shape[0]
    for place, block in enumerate(blocks[:-1]):
        out[place * count : place * count + count] = block[...]


def position_of(offset):
    slot = jnp.int32(0)
    for index in range(1, 8):
        slot = jnp.where(offset == RING8[index], index, slot)
    return slot


def add_products(offsets, responses, padded, band, rows_f32, total):
    rcv = lax.axis_index("rcv")
    y, z = rcv // 8, rcv % 8
    slots = [position_of((sign(z) * (wanted - z) + 64) % 8) for wanted in range(8)]
    for response, offset in zip(responses, offsets, strict=True):
        for half in range(2):
            for q in range(4):
                piece = response[slots[half * 4 + q]]
                rows_f32[half, q * 64 : q * 64 + 64, :] = piece.astype(jnp.float32)
            wide = jnp.concatenate(
                [rows_f32[half, pl.ds(m, 16, stride=16), :] for m in range(16)]
                + [jnp.zeros((16, 384), jnp.float32)],
                axis=1,
            )
            for shift in range(4):
                band[half, shift * 16 : shift * 16 + 16, :] = pltpu.roll(
                    wide, 128 + 32 * shift, 1
                ).astype(jnp.bfloat16)
        place = ((y + 4 - offset) % 4) * 2
        even_rows, odd_rows, sides = [], [], []
        for group in range(5):
            sides += [
                padded[place + half, 64 - 16 * group : 576 - 16 * group, :] for half in range(2)
            ]
            for rows, step in ((even_rows, 2 * group), (odd_rows, 2 * group + 1)):
                if step <= 8:
                    for half in range(2):
                        for late in range(2):
                            first = (2 * step - late + 1) * 128
                            rows.append(band[half, :, first : first + 256])
        total[...] += jnp.dot(
            jnp.concatenate(sides, axis=1),
            jnp.concatenate(even_rows, axis=0),
            preferred_element_type=jnp.float32,
        )
        odd = jnp.dot(
            jnp.concatenate(sides[:8], axis=1),
            jnp.concatenate(odd_rows, axis=0),
            preferred_element_type=jnp.float32,
        )
        total[8:, :] += odd[:504, :]


def first_kernel(own, padded, total, band, rows):
    total[...] = jnp.zeros_like(total)
    add_products((0,), (own,), padded, band, rows, total)


def middle_kernel(offset, response, padded, so_far, total, band, rows):
    total[...] = so_far[...]
    add_products((offset,), (response,), padded, band, rows, total)


def last_kernel(across, padded, so_far, out, band, rows, total, placed):
    total[...] = so_far[...]
    add_products((2,), (across,), padded, band, rows, total)
    turned = total[...].T
    skewed = [pltpu.roll(turned[u * 32 : u * 32 + 32, :], u, 1) for u in range(8)]
    lane = lax.broadcasted_iota(jnp.int32, (32, 512), 1)
    for r in range(8):
        mixed = skewed[0]
        for u in range(1, 8):
            mixed = jnp.where(lane % 8 == (r + u) % 8, skewed[u], mixed)
        mixed = pltpu.roll(mixed, (512 - r) % 512, 1)
        for part in range(4):
            placed[part, pl.ds(r, 32, stride=8), :] = mixed[:, part * 128 : part * 128 + 128]
    for part in range(4):
        out[:, :, part * 128 : part * 128 + 128] = placed[part].reshape(32, 8, 128).astype(jnp.bfloat16)


def call(body, shape, dtype, operands, scratch, flops=0):
    return pl.pallas_call(
        body,
        out_shape=jax.ShapeDtypeStruct(shape, dtype),
        in_specs=[VMEM] * len(operands),
        out_specs=VMEM,
        scratch_shapes=[pltpu.VMEM(s, d) for s, d in scratch],
        compiler_params=PARAMS,
        cost_estimate=pl.CostEstimate(flops=flops, bytes_accessed=2**20, transcendentals=0),
    )(*operands)


def shards(response, traces):
    f32, bf16 = jnp.float32, jnp.bfloat16
    band = [((2, 64, 19 * 128), bf16), ((2, 256, 128), f32)]

    def along_z(step):
        return lambda i: (i // 8) * 8 + step(i % 8) % 8

    def along_y(offset):
        return lambda i: (i // 8 + offset) % 4 * 8 + i % 8

    def along_x(i):
        return ((i // 2 + sign(i)) % 4) * 2 + i % 2

    def across_x(i):
        return (i + 4) % 8

    def swap(value):
        return spread(value, "shot", lambda i: i ^ 1)

    held = call(
        prepare_response,
        (64, 128),
        bf16,
        (response.reshape(128, 64),),
        [((128, 128), f32), ((64, 128), f32)],
    )
    held = held[None]
    both = call(
        prepare_traces,
        (2, 512, 128),
        bf16,
        (traces, swap(traces), held),
        [((2, 4, 128, 128), f32), ((2, 512, 128), f32)],
    )
    held = call(join, (2, 64, 128), bf16, (held, spread(held, "rcv", along_z(lambda z: z + sign(z)))), [], JOIN_COST)
    arrived = [
        spread(held, "rcv", along_z(lambda z, hops=hops: z - hops * sign(z))) for hops in (3, 2, 1)
    ]
    held = call(join, (8, 64, 128), bf16, (held, *arrived), [], JOIN_COST)
    before, after, across = [spread(held, "rcv", along_y(offset)) for offset in (1, 3, 2)]

    near = spread(both, "shot", along_x)
    far = spread(both[0], "shot", across_x)
    pieces = (both, near, swap(near), far, swap(far))
    padded = call(assemble, (8, 576, 128), bf16, pieces, [])
    work = 2 * 512 * 256 * 9 * 256
    total = call(first_kernel, (512, 256), f32, (held, padded), band, work)
    for offset, block in ((3, after), (1, before)):
        body = functools.partial(middle_kernel, offset)
        total = call(body, (512, 256), f32, (block, padded, total), band, work)
    return call(
        last_kernel,
        (32, 8, 512),
        bf16,
        (across, padded, total),
        band + [((512, 256), f32), ((4, 256, 128), f32)],
        work,
    )


def solution(mesh):
    placed = (P("shot", "rcv", None), P("shot", "rcv", None))
    return jax.shard_map(
        shards, mesh=mesh, in_specs=placed, out_specs=P("shot", "rcv", None), check_vma=False
    )
```

```python
import functools

import jax
import jax.numpy as jnp
from jax import lax
from jax.experimental import pallas as pl
from jax.experimental.pallas import tpu as pltpu
from jax.sharding import PartitionSpec as P

RING8 = (0, 1, 5, 4, 2, 3, 7, 6)
VMEM = pl.BlockSpec(memory_space=pltpu.VMEM)
JOIN_COST = 2**33
PARAMS = pltpu.CompilerParams(vmem_limit_bytes=40 * 2**20)


def spread(value, axis, partner):
    size = lax.axis_size(axis)
    return lax.ppermute(value, axis, [(i, partner(i)) for i in range(size)])


def sign(coordinate):
    return 1 - 2 * (coordinate % 2)


def prepare_response(response, out, rows, turned):
    wide = response[...].astype(jnp.float32)
    rows[...] = jnp.concatenate([wide, jnp.zeros((128, 64), jnp.float32)], axis=1)
    by_position = jnp.concatenate([rows[pl.ds(k, 32, stride=4), :] for k in range(4)], axis=0)
    turned[...] = by_position.T[:64, :]
    skewed = [pltpu.roll(turned[pl.ds(u, 16, stride=4), :], 32 * u, 1) for u in range(4)]
    lane_block = lax.broadcasted_iota(jnp.int32, (16, 128), 1) // 32
    for k in range(4):
        mixed = skewed[0]
        for u in range(1, 4):
            mixed = jnp.where(lane_block == (k + u) % 4, skewed[u], mixed)
        out[k * 16 : k * 16 + 16, :] = pltpu.roll(mixed, (128 - 32 * k) % 128, 1).astype(jnp.bfloat16)


def prepare_traces(own, other, _, out, rows, turned):
    lane_block = lax.broadcasted_iota(jnp.int32, (64, 128), 1) // 16
    for side, traces in enumerate((own, other)):
        for part in range(4):
            lanes = traces[:, :, part * 128 : part * 128 + 128]
            rows[side, part] = lanes.astype(jnp.float32).reshape(128, 128)
        for part in range(4):
            by_receiver = [rows[side, part, pl.ds(r, 16, stride=8), :] for r in range(8)]
            turned[side, part * 128 : part * 128 + 128, :] = jnp.concatenate(by_receiver, axis=0).T
        skewed = [pltpu.roll(turned[side, pl.ds(d, 64, stride=8), :], 16 * d, 1) for d in range(8)]
        for r in range(8):
            mixed = skewed[0]
            for d in range(1, 8):
                mixed = jnp.where(lane_block == (r + d) % 8, skewed[d], mixed)
            turned[side, pl.ds(r, 64, stride=8), :] = pltpu.roll(mixed, (128 - 16 * r) % 128, 1)
        out[side] = turned[side].astype(jnp.bfloat16)


def assemble(own, near, near_swapped, far, out):
    shot = lax.axis_index("shot")
    x, core = shot // 2, shot % 2
    back = 4 - sign(core)
    blocks = (
        (own.at[0], x, core),
        (own.at[1], x, 1 - core),
        (near.at[0], x + back, core),
        (near.at[1], x + back, 1 - core),
        (near_swapped.at[0], x + 8 - back, 1 - core),
        (near_swapped.at[1], x + 8 - back, core),
        (far.at[0], x + 2, core),
        (far.at[1], x + 2, 1 - core),
    )
    for block, chip, side in blocks:
        place = (chip % 4) * 2 + side
        out[place, :64, :] = jnp.zeros((64, 128), jnp.bfloat16)
        out[place, 64:, :] = block[...]


def join(*blocks):
    out = blocks[-1]
    count = blocks[0].shape[0]
    for place, block in enumerate(blocks[:-1]):
        out[place * count : place * count + count] = block[...]


def position_of(offset):
    slot = jnp.int32(0)
    for index in range(1, 8):
        slot = jnp.where(offset == RING8[index], index, slot)
    return slot


def add_products(offsets, responses, padded, band, rows_f32, total):
    rcv = lax.axis_index("rcv")
    y, z = rcv // 8, rcv % 8
    slots = [position_of((sign(z) * (wanted - z) + 64) % 8) for wanted in range(8)]
    for response, offset in zip(responses, offsets, strict=True):
        for half in range(2):
            for q in range(4):
                piece = response[slots[half * 4 + q]]
                rows_f32[half, q * 64 : q * 64 + 64, :] = piece.astype(jnp.float32)
            wide = jnp.concatenate(
                [rows_f32[half, pl.ds(m, 16, stride=16), :] for m in range(16)]
                + [jnp.zeros((16, 384), jnp.float32)],
                axis=1,
            )
            for shift in range(4):
                band[half, shift * 16 : shift * 16 + 16, :] = pltpu.roll(
                    wide, 128 + 32 * shift, 1
                ).astype(jnp.bfloat16)
        place = ((y + 4 - offset) % 4) * 2
        even_rows, odd_rows, sides = [], [], []
        for group in range(5):
            sides += [
                padded[place + half, 64 - 16 * group : 576 - 16 * group, :] for half in range(2)
            ]
            for rows, step in ((even_rows, 2 * group), (odd_rows, 2 * group + 1)):
                if step <= 8:
                    for half in range(2):
                        for late in range(2):
                            first = (2 * step - late + 1) * 128
                            rows.append(band[half, :, first : first + 256])
        total[...] += jnp.dot(
            jnp.concatenate(sides, axis=1),
            jnp.concatenate(even_rows, axis=0),
            preferred_element_type=jnp.float32,
        )
        odd = jnp.dot(
            jnp.concatenate(sides[:8], axis=1),
            jnp.concatenate(odd_rows, axis=0),
            preferred_element_type=jnp.float32,
        )
        total[8:, :] += odd[:504, :]


def first_kernel(own, padded, total, band, rows):
    total[...] = jnp.zeros_like(total)
    add_products((0,), (own,), padded, band, rows, total)


def middle_kernel(offset, response, padded, so_far, total, band, rows):
    total[...] = so_far[...]
    add_products((offset,), (response,), padded, band, rows, total)


def last_kernel(across, padded, so_far, out, band, rows, total, placed):
    total[...] = so_far[...]
    add_products((2,), (across,), padded, band, rows, total)
    turned = total[...].T
    skewed = [pltpu.roll(turned[u * 32 : u * 32 + 32, :], u, 1) for u in range(8)]
    lane = lax.broadcasted_iota(jnp.int32, (32, 512), 1)
    for r in range(8):
        mixed = skewed[0]
        for u in range(1, 8):
            mixed = jnp.where(lane % 8 == (r + u) % 8, skewed[u], mixed)
        mixed = pltpu.roll(mixed, (512 - r) % 512, 1)
        for part in range(4):
            placed[part, pl.ds(r, 32, stride=8), :] = mixed[:, part * 128 : part * 128 + 128]
    for part in range(4):
        out[:, :, part * 128 : part * 128 + 128] = placed[part].reshape(32, 8, 128).astype(jnp.bfloat16)


def call(body, shape, dtype, operands, scratch, flops=0):
    return pl.pallas_call(
        body,
        out_shape=jax.ShapeDtypeStruct(shape, dtype),
        in_specs=[VMEM] * len(operands),
        out_specs=VMEM,
        scratch_shapes=[pltpu.VMEM(s, d) for s, d in scratch],
        compiler_params=PARAMS,
        cost_estimate=pl.CostEstimate(flops=flops, bytes_accessed=2**20, transcendentals=0),
    )(*operands)


def shards(response, traces):
    f32, bf16 = jnp.float32, jnp.bfloat16
    band = [((2, 64, 19 * 128), bf16), ((2, 256, 128), f32)]

    def along_z(step):
        return lambda i: (i // 8) * 8 + step(i % 8) % 8

    def along_y(offset):
        return lambda i: (i // 8 + offset) % 4 * 8 + i % 8

    def along_x(i):
        return ((i // 2 + sign(i)) % 4) * 2 + i % 2

    def across_x(i):
        return (i + 4) % 8

    def swap(value):
        return spread(value, "shot", lambda i: i ^ 1)

    held = call(
        prepare_response,
        (64, 128),
        bf16,
        (response.reshape(128, 64),),
        [((128, 128), f32), ((64, 128), f32)],
    )
    held = held[None]
    both = call(
        prepare_traces,
        (2, 512, 128),
        bf16,
        (traces, swap(traces), held),
        [((2, 4, 128, 128), f32), ((2, 512, 128), f32)],
    )
    held = call(join, (2, 64, 128), bf16, (held, spread(held, "rcv", along_z(lambda z: z + sign(z)))), [], JOIN_COST)
    arrived = [
        spread(held, "rcv", along_z(lambda z, hops=hops: z - hops * sign(z))) for hops in (3, 2, 1)
    ]
    held = call(join, (8, 64, 128), bf16, (held, *arrived), [], JOIN_COST)
    before, after, across = [spread(held, "rcv", along_y(offset)) for offset in (1, 3, 2)]

    near = spread(both, "shot", along_x)
    far = spread(both, "shot", across_x)
    pieces = (both, near, swap(near), far)
    padded = call(assemble, (8, 576, 128), bf16, pieces, [])
    work = 2 * 512 * 256 * 9 * 256
    total = call(first_kernel, (512, 256), f32, (held, padded), band, work)
    for offset, block in ((3, after), (1, before)):
        body = functools.partial(middle_kernel, offset)
        total = call(body, (512, 256), f32, (block, padded, total), band, work)
    return call(
        last_kernel,
        (32, 8, 512),
        bf16,
        (across, padded, total),
        band + [((512, 256), f32), ((4, 256, 128), f32)],
        work,
    )


def solution(mesh):
    placed = (P("shot", "rcv", None), P("shot", "rcv", None))
    return jax.shard_map(
        shards, mesh=mesh, in_specs=placed, out_specs=P("shot", "rcv", None), check_vma=False
    )
```

```python
import functools

import jax
import jax.numpy as jnp
from jax import lax
from jax.experimental import pallas as pl
from jax.experimental.pallas import tpu as pltpu
from jax.sharding import PartitionSpec as P

RING8 = (0, 1, 5, 4, 2, 3, 7, 6)
VMEM = pl.BlockSpec(memory_space=pltpu.VMEM)
JOIN_COST = 2**33
PARAMS = pltpu.CompilerParams(vmem_limit_bytes=40 * 2**20)


def spread(value, axis, partner):
    size = lax.axis_size(axis)
    return lax.ppermute(value, axis, [(i, partner(i)) for i in range(size)])


def sign(coordinate):
    return 1 - 2 * (coordinate % 2)


def prepare_response(response, out, rows, turned):
    wide = response[...].astype(jnp.float32)
    rows[...] = jnp.concatenate([wide, jnp.zeros((128, 64), jnp.float32)], axis=1)
    by_position = jnp.concatenate([rows[pl.ds(k, 32, stride=4), :] for k in range(4)], axis=0)
    turned[...] = by_position.T[:64, :]
    skewed = [pltpu.roll(turned[pl.ds(u, 16, stride=4), :], 32 * u, 1) for u in range(4)]
    lane_block = lax.broadcasted_iota(jnp.int32, (16, 128), 1) // 32
    for k in range(4):
        mixed = skewed[0]
        for u in range(1, 4):
            mixed = jnp.where(lane_block == (k + u) % 4, skewed[u], mixed)
        out[k * 16 : k * 16 + 16, :] = pltpu.roll(mixed, (128 - 32 * k) % 128, 1).astype(jnp.bfloat16)


def prepare_traces(own, other, _, out, rows, turned):
    lane_block = lax.broadcasted_iota(jnp.int32, (64, 128), 1) // 16
    for side, traces in enumerate((own, other)):
        for part in range(4):
            lanes = traces[:, :, part * 128 : part * 128 + 128]
            rows[side, part] = lanes.astype(jnp.float32).reshape(128, 128)
        for part in range(4):
            by_receiver = [rows[side, part, pl.ds(r, 16, stride=8), :] for r in range(8)]
            turned[side, part * 128 : part * 128 + 128, :] = jnp.concatenate(by_receiver, axis=0).T
        skewed = [pltpu.roll(turned[side, pl.ds(d, 64, stride=8), :], 16 * d, 1) for d in range(8)]
        for r in range(8):
            mixed = skewed[0]
            for d in range(1, 8):
                mixed = jnp.where(lane_block == (r + d) % 8, skewed[d], mixed)
            turned[side, pl.ds(r, 64, stride=8), :] = pltpu.roll(mixed, (128 - 16 * r) % 128, 1)
        out[side] = turned[side].astype(jnp.bfloat16)


def assemble(own, near, near_swapped, far, out):
    shot = lax.axis_index("shot")
    x, core = shot // 2, shot % 2
    back = 4 - sign(core)
    blocks = (
        (own.at[0], x, core),
        (own.at[1], x, 1 - core),
        (near.at[0], x + back, core),
        (near.at[1], x + back, 1 - core),
        (near_swapped.at[0], x + 8 - back, 1 - core),
        (near_swapped.at[1], x + 8 - back, core),
        (far.at[0], x + 2, core),
        (far.at[1], x + 2, 1 - core),
    )
    for block, chip, side in blocks:
        place = (chip % 4) * 2 + side
        out[place, :64, :] = jnp.zeros((64, 128), jnp.bfloat16)
        out[place, 64:, :] = block[...]


def join(*blocks):
    out = blocks[-1]
    count = blocks[0].shape[0]
    for place, block in enumerate(blocks[:-1]):
        out[place * count : place * count + count] = block[...]


def position_of(offset):
    slot = jnp.int32(0)
    for index in range(1, 8):
        slot = jnp.where(offset == RING8[index], index, slot)
    return slot


def add_products(offsets, responses, padded, band, rows_f32, total):
    rcv = lax.axis_index("rcv")
    y, z = rcv // 8, rcv % 8
    slots = [position_of((sign(z) * (wanted - z) + 64) % 8) for wanted in range(8)]
    for response, offset in zip(responses, offsets, strict=True):
        for half in range(2):
            for q in range(4):
                piece = response[slots[half * 4 + q]]
                rows_f32[half, q * 64 : q * 64 + 64, :] = piece.astype(jnp.float32)
            wide = jnp.concatenate(
                [rows_f32[half, pl.ds(m, 16, stride=16), :] for m in range(16)]
                + [jnp.zeros((16, 384), jnp.float32)],
                axis=1,
            )
            for shift in range(4):
                band[half, shift * 16 : shift * 16 + 16, :] = pltpu.roll(
                    wide, 128 + 32 * shift, 1
                ).astype(jnp.bfloat16)
        place = ((y + 4 - offset) % 4) * 2
        even_rows, odd_rows, sides = [], [], []
        for group in range(5):
            sides += [
                padded[place + half, 64 - 16 * group : 576 - 16 * group, :] for half in range(2)
            ]
            for rows, step in ((even_rows, 2 * group), (odd_rows, 2 * group + 1)):
                if step <= 8:
                    for half in range(2):
                        for late in range(2):
                            first = (2 * step - late + 1) * 128
                            rows.append(band[half, :, first : first + 256])
        total[...] += jnp.dot(
            jnp.concatenate(sides, axis=1),
            jnp.concatenate(even_rows, axis=0),
            preferred_element_type=jnp.float32,
        )
        odd = jnp.dot(
            jnp.concatenate(sides[:8], axis=1),
            jnp.concatenate(odd_rows, axis=0),
            preferred_element_type=jnp.float32,
        )
        total[8:, :] += odd[:504, :]


def first_kernel(own, padded, total, band, rows):
    total[...] = jnp.zeros_like(total)
    add_products((0,), (own,), padded, band, rows, total)


def middle_kernel(offset, response, padded, so_far, total, band, rows):
    total[...] = so_far[...]
    add_products((offset,), (response,), padded, band, rows, total)


def last_kernel(before, padded, so_far, out, band, rows, total, placed):
    total[...] = so_far[...]
    add_products((1,), (before,), padded, band, rows, total)
    turned = total[...].T
    skewed = [pltpu.roll(turned[u * 32 : u * 32 + 32, :], u, 1) for u in range(8)]
    lane = lax.broadcasted_iota(jnp.int32, (32, 512), 1)
    for r in range(8):
        mixed = skewed[0]
        for u in range(1, 8):
            mixed = jnp.where(lane % 8 == (r + u) % 8, skewed[u], mixed)
        mixed = pltpu.roll(mixed, (512 - r) % 512, 1)
        for part in range(4):
            placed[part, pl.ds(r, 32, stride=8), :] = mixed[:, part * 128 : part * 128 + 128]
    for part in range(4):
        out[:, :, part * 128 : part * 128 + 128] = placed[part].reshape(32, 8, 128).astype(jnp.bfloat16)


def call(body, shape, dtype, operands, scratch, flops=0):
    return pl.pallas_call(
        body,
        out_shape=jax.ShapeDtypeStruct(shape, dtype),
        in_specs=[VMEM] * len(operands),
        out_specs=VMEM,
        scratch_shapes=[pltpu.VMEM(s, d) for s, d in scratch],
        compiler_params=PARAMS,
        cost_estimate=pl.CostEstimate(flops=flops, bytes_accessed=2**20, transcendentals=0),
    )(*operands)


def shards(response, traces):
    f32, bf16 = jnp.float32, jnp.bfloat16
    band = [((2, 64, 19 * 128), bf16), ((2, 256, 128), f32)]

    def along_z(step):
        return lambda i: (i // 8) * 8 + step(i % 8) % 8

    def along_y(offset):
        return lambda i: (i // 8 + offset) % 4 * 8 + i % 8

    def along_x(i):
        return ((i // 2 + sign(i)) % 4) * 2 + i % 2

    def across_x(i):
        return (i + 4) % 8

    def swap(value):
        return spread(value, "shot", lambda i: i ^ 1)

    held = call(
        prepare_response,
        (64, 128),
        bf16,
        (response.reshape(128, 64),),
        [((128, 128), f32), ((64, 128), f32)],
    )
    held = held[None]
    both = call(
        prepare_traces,
        (2, 512, 128),
        bf16,
        (traces, swap(traces), held),
        [((2, 4, 128, 128), f32), ((2, 512, 128), f32)],
    )
    held = call(join, (2, 64, 128), bf16, (held, spread(held, "rcv", along_z(lambda z: z + sign(z)))), [], JOIN_COST)
    arrived = [
        spread(held, "rcv", along_z(lambda z, hops=hops: z - hops * sign(z))) for hops in (3, 2, 1)
    ]
    held = call(join, (8, 64, 128), bf16, (held, *arrived), [], JOIN_COST)
    before, after, across = [spread(held, "rcv", along_y(offset)) for offset in (1, 3, 2)]

    near = spread(both, "shot", along_x)
    far = spread(both, "shot", across_x)
    pieces = (both, near, swap(near), far)
    padded = call(assemble, (8, 576, 128), bf16, pieces, [])
    work = 2 * 512 * 256 * 9 * 256
    total = call(first_kernel, (512, 256), f32, (held, padded), band, work)
    for offset, block in ((2, across), (3, after)):
        body = functools.partial(middle_kernel, offset)
        total = call(body, (512, 256), f32, (block, padded, total), band, work)
    return call(
        last_kernel,
        (32, 8, 512),
        bf16,
        (before, padded, total),
        band + [((512, 256), f32), ((4, 256, 128), f32)],
        work,
    )


def solution(mesh):
    placed = (P("shot", "rcv", None), P("shot", "rcv", None))
    return jax.shard_map(
        shards, mesh=mesh, in_specs=placed, out_specs=P("shot", "rcv", None), check_vma=False
    )
```

```python
import functools

import jax
import jax.numpy as jnp
from jax import lax
from jax.experimental import pallas as pl
from jax.experimental.pallas import tpu as pltpu
from jax.sharding import PartitionSpec as P

RING8 = (0, 1, 2, 3, 7, 6, 5, 4)
VMEM = pl.BlockSpec(memory_space=pltpu.VMEM)
JOIN_COST = 2**33
PARAMS = pltpu.CompilerParams(vmem_limit_bytes=40 * 2**20)


def spread(value, axis, partner):
    size = lax.axis_size(axis)
    return lax.ppermute(value, axis, [(i, partner(i)) for i in range(size)])


def sign(coordinate):
    return 1 - 2 * (coordinate % 2)


def prepare_response(response, out, rows, turned):
    wide = response[...].astype(jnp.float32)
    rows[...] = jnp.concatenate([wide, jnp.zeros((128, 64), jnp.float32)], axis=1)
    by_position = jnp.concatenate([rows[pl.ds(k, 32, stride=4), :] for k in range(4)], axis=0)
    turned[...] = by_position.T[:64, :]
    skewed = [pltpu.roll(turned[pl.ds(u, 16, stride=4), :], 32 * u, 1) for u in range(4)]
    lane_block = lax.broadcasted_iota(jnp.int32, (16, 128), 1) // 32
    for k in range(4):
        mixed = skewed[0]
        for u in range(1, 4):
            mixed = jnp.where(lane_block == (k + u) % 4, skewed[u], mixed)
        out[k * 16 : k * 16 + 16, :] = pltpu.roll(mixed, (128 - 32 * k) % 128, 1).astype(jnp.bfloat16)


def prepare_traces(own, other, _, out, rows, turned):
    lane_block = lax.broadcasted_iota(jnp.int32, (64, 128), 1) // 16
    for side, traces in enumerate((own, other)):
        for part in range(4):
            lanes = traces[:, :, part * 128 : part * 128 + 128]
            rows[side, part] = lanes.astype(jnp.float32).reshape(128, 128)
        for part in range(4):
            by_receiver = [rows[side, part, pl.ds(r, 16, stride=8), :] for r in range(8)]
            turned[side, part * 128 : part * 128 + 128, :] = jnp.concatenate(by_receiver, axis=0).T
        skewed = [pltpu.roll(turned[side, pl.ds(d, 64, stride=8), :], 16 * d, 1) for d in range(8)]
        for r in range(8):
            mixed = skewed[0]
            for d in range(1, 8):
                mixed = jnp.where(lane_block == (r + d) % 8, skewed[d], mixed)
            turned[side, pl.ds(r, 64, stride=8), :] = pltpu.roll(mixed, (128 - 16 * r) % 128, 1)
        out[side] = turned[side].astype(jnp.bfloat16)


def assemble(own, near, near_swapped, far, out):
    shot = lax.axis_index("shot")
    x, core = shot // 2, shot % 2
    back = 4 - sign(core)
    blocks = (
        (own.at[0], x, core),
        (own.at[1], x, 1 - core),
        (near.at[0], x + back, core),
        (near.at[1], x + back, 1 - core),
        (near_swapped.at[0], x + 8 - back, 1 - core),
        (near_swapped.at[1], x + 8 - back, core),
        (far.at[0], x + 2, core),
        (far.at[1], x + 2, 1 - core),
    )
    for block, chip, side in blocks:
        place = (chip % 4) * 2 + side
        out[place, :64, :] = jnp.zeros((64, 128), jnp.bfloat16)
        out[place, 64:, :] = block[...]


def join(*blocks):
    out = blocks[-1]
    count = blocks[0].shape[0]
    for place, block in enumerate(blocks[:-1]):
        out[place * count : place * count + count] = block[...]


def position_of(offset):
    slot = jnp.int32(0)
    for index in range(1, 8):
        slot = jnp.where(offset == RING8[index], index, slot)
    return slot


def add_products(offset, response, padded, band, rows_f32, so_far, total):
    rcv = lax.axis_index("rcv")
    y, z = rcv // 8, rcv % 8
    slots = [position_of((sign(z) * (wanted - z) + 64) % 8) for wanted in range(8)]
    for half in range(2):
        for q in range(4):
            piece = response[slots[half * 4 + q]]
            rows_f32[half, q * 64 : q * 64 + 64, :] = piece.astype(jnp.float32)
        wide = jnp.concatenate(
            [rows_f32[half, pl.ds(m, 16, stride=16), :] for m in range(16)]
            + [jnp.zeros((16, 384), jnp.float32)],
            axis=1,
        )
        for shift in range(4):
            band[half, shift * 16 : shift * 16 + 16, :] = pltpu.roll(
                wide, 128 + 32 * shift, 1
            ).astype(jnp.bfloat16)
    place = ((y + 4 - offset) % 4) * 2
    even_rows, odd_rows, sides = [], [], []
    for group in range(5):
        sides += [
            padded[place + half, 64 - 16 * group : 576 - 16 * group, :] for half in range(2)
        ]
        for rows, step in ((even_rows, 2 * group), (odd_rows, 2 * group + 1)):
            if step <= 8:
                for half in range(2):
                    for late in range(2):
                        first = (2 * step - late + 1) * 128
                        rows.append(band[half, :, first : first + 256])
    even = jnp.dot(
        jnp.concatenate(sides, axis=1),
        jnp.concatenate(even_rows, axis=0),
        preferred_element_type=jnp.float32,
    )
    odd = jnp.dot(
        jnp.concatenate(sides[:8], axis=1),
        jnp.concatenate(odd_rows, axis=0),
        preferred_element_type=jnp.float32,
    )
    if so_far is None:
        total[:8, :] = even[:8, :]
        total[8:, :] = even[8:, :] + odd[:504, :]
    else:
        total[:8, :] = so_far[:8, :] + even[:8, :]
        total[8:, :] = so_far[8:, :] + even[8:, :] + odd[:504, :]


def first_kernel(own, padded, total, band, rows):
    add_products(0, own, padded, band, rows, None, total)


def middle_kernel(offset, response, padded, so_far, total, band, rows):
    add_products(offset, response, padded, band, rows, so_far, total)


def last_kernel(before, padded, so_far, out, band, rows, total, placed):
    add_products(1, before, padded, band, rows, so_far, total)
    turned = total[...].astype(jnp.bfloat16).T
    turned = turned.astype(jnp.bfloat16)
    skewed = [pltpu.roll(turned[u * 32 : u * 32 + 32, :], u, 1) for u in range(8)]
    lane = lax.broadcasted_iota(jnp.int32, (32, 512), 1)
    for r in range(8):
        mixed = skewed[0]
        for u in range(1, 8):
            mixed = jnp.where(lane % 8 == (r + u) % 8, skewed[u], mixed)
        mixed = pltpu.roll(mixed, (512 - r) % 512, 1)
        for part in range(4):
            placed[part, pl.ds(r, 32, stride=8), :] = mixed[:, part * 128 : part * 128 + 128].astype(jnp.float32)
    for part in range(4):
        out[:, :, part * 128 : part * 128 + 128] = placed[part].reshape(32, 8, 128).astype(jnp.bfloat16)


def call(body, shape, dtype, operands, scratch, flops=0):
    return pl.pallas_call(
        body,
        out_shape=jax.ShapeDtypeStruct(shape, dtype),
        in_specs=[VMEM] * len(operands),
        out_specs=VMEM,
        scratch_shapes=[pltpu.VMEM(s, d) for s, d in scratch],
        compiler_params=PARAMS,
        cost_estimate=pl.CostEstimate(flops=flops, bytes_accessed=2**20, transcendentals=0),
    )(*operands)


def shards(response, traces):
    f32, bf16 = jnp.float32, jnp.bfloat16
    band = [((2, 64, 19 * 128), bf16), ((2, 256, 128), f32)]

    def along_z(step):
        return lambda i: (i // 8) * 8 + step(i % 8) % 8

    def along_y(offset):
        return lambda i: (i // 8 + offset) % 4 * 8 + i % 8

    def along_x(i):
        return ((i // 2 + sign(i)) % 4) * 2 + i % 2

    def across_x(i):
        return (i + 4) % 8

    def swap(value):
        return spread(value, "shot", lambda i: i ^ 1)

    held = call(
        prepare_response,
        (64, 128),
        bf16,
        (response.reshape(128, 64),),
        [((128, 128), f32), ((64, 128), f32)],
    )
    held = held[None]
    both = call(
        prepare_traces,
        (2, 512, 128),
        bf16,
        (traces, swap(traces), held),
        [((2, 4, 128, 128), f32), ((2, 512, 128), f32)],
    )
    for step in (lambda z: z + sign(z), lambda z: z - 2 * sign(z), lambda z: z - sign(z)):
        arrived = spread(held, "rcv", along_z(step))
        held = call(join, (2 * held.shape[0], 64, 128), bf16, (held, arrived), [], JOIN_COST)
    before, after, across = [spread(held, "rcv", along_y(offset)) for offset in (1, 3, 2)]

    near = spread(both, "shot", along_x)
    far = spread(both, "shot", across_x)
    pieces = (both, near, swap(near), far)
    padded = call(assemble, (8, 576, 128), bf16, pieces, [])
    work = 2 * 512 * 256 * 9 * 256
    total = call(first_kernel, (512, 256), f32, (held, padded), band, work)
    for offset, block in ((2, across), (3, after)):
        body = functools.partial(middle_kernel, offset)
        total = call(body, (512, 256), f32, (block, padded, total), band, work)
    return call(
        last_kernel,
        (32, 8, 512),
        bf16,
        (before, padded, total),
        band + [((512, 256), f32), ((4, 256, 128), f32)],
        work,
    )


def solution(mesh):
    placed = (P("shot", "rcv", None), P("shot", "rcv", None))
    return jax.shard_map(
        shards, mesh=mesh, in_specs=placed, out_specs=P("shot", "rcv", None), check_vma=False
    )
```

```python
import functools

import jax
import jax.numpy as jnp
from jax import lax
from jax.experimental import pallas as pl
from jax.experimental.pallas import tpu as pltpu
from jax.sharding import PartitionSpec as P

RING8 = (0, 1, 5, 4, 2, 3, 7, 6)
VMEM = pl.BlockSpec(memory_space=pltpu.VMEM)
JOIN_COST = 2**33
PARAMS = pltpu.CompilerParams(vmem_limit_bytes=40 * 2**20)


def spread(value, axis, partner):
    size = lax.axis_size(axis)
    return lax.ppermute(value, axis, [(i, partner(i)) for i in range(size)])


def sign(coordinate):
    return 1 - 2 * (coordinate % 2)


def prepare_responses(own, neighbour, out, rows, turned):
    lane_block = lax.broadcasted_iota(jnp.int32, (16, 128), 1) // 32
    for side, response in enumerate((own, neighbour)):
        wide = response[...].astype(jnp.float32)
        rows[side] = jnp.concatenate([wide, jnp.zeros((128, 64), jnp.float32)], axis=1)
        by_position = [rows[side, pl.ds(k, 32, stride=4), :] for k in range(4)]
        turned[side] = jnp.concatenate(by_position, axis=0).T[:64, :]
        skewed = [pltpu.roll(turned[side, pl.ds(u, 16, stride=4), :], 32 * u, 1) for u in range(4)]
        for k in range(4):
            mixed = skewed[0]
            for u in range(1, 4):
                mixed = jnp.where(lane_block == (k + u) % 4, skewed[u], mixed)
            mixed = pltpu.roll(mixed, (128 - 32 * k) % 128, 1)
            out[side, k * 16 : k * 16 + 16, :] = mixed.astype(jnp.bfloat16)


def prepare_traces(own, other, out, rows, turned):
    lane_block = lax.broadcasted_iota(jnp.int32, (64, 128), 1) // 16
    for side, traces in enumerate((own, other)):
        for part in range(4):
            lanes = traces[:, :, part * 128 : part * 128 + 128]
            rows[side, part] = lanes.astype(jnp.float32).reshape(128, 128)
        for part in range(4):
            by_receiver = [rows[side, part, pl.ds(r, 16, stride=8), :] for r in range(8)]
            turned[side, part * 128 : part * 128 + 128, :] = jnp.concatenate(by_receiver, axis=0).T
        skewed = [pltpu.roll(turned[side, pl.ds(d, 64, stride=8), :], 16 * d, 1) for d in range(8)]
        for r in range(8):
            mixed = skewed[0]
            for d in range(1, 8):
                mixed = jnp.where(lane_block == (r + d) % 8, skewed[d], mixed)
            turned[side, pl.ds(r, 64, stride=8), :] = pltpu.roll(mixed, (128 - 16 * r) % 128, 1)
        out[side] = turned[side].astype(jnp.bfloat16)


def assemble(own, near, near_swapped, far, out):
    shot = lax.axis_index("shot")
    x, core = shot // 2, shot % 2
    back = 4 - sign(core)
    blocks = (
        (own.at[0], x, core),
        (own.at[1], x, 1 - core),
        (near.at[0], x + back, core),
        (near.at[1], x + back, 1 - core),
        (near_swapped.at[0], x + 8 - back, 1 - core),
        (near_swapped.at[1], x + 8 - back, core),
        (far.at[0], x + 2, core),
        (far.at[1], x + 2, 1 - core),
    )
    for block, chip, side in blocks:
        place = (chip % 4) * 2 + side
        out[place, :64, :] = jnp.zeros((64, 128), jnp.bfloat16)
        out[place, 64:, :] = block[...]


def join(*blocks):
    out = blocks[-1]
    count = blocks[0].shape[0]
    for place, block in enumerate(blocks[:-1]):
        out[place * count : place * count + count] = block[...]


def position_of(offset):
    slot = jnp.int32(0)
    for index in range(1, 8):
        slot = jnp.where(offset == RING8[index], index, slot)
    return slot


def add_products(offset, response, padded, band, rows_f32, so_far, total):
    rcv = lax.axis_index("rcv")
    y, z = rcv // 8, rcv % 8
    slots = [position_of((sign(z) * (wanted - z) + 64) % 8) for wanted in range(8)]
    for half in range(2):
        for q in range(4):
            piece = response[slots[half * 4 + q]]
            rows_f32[half, q * 64 : q * 64 + 64, :] = piece.astype(jnp.float32)
        wide = jnp.concatenate(
            [rows_f32[half, pl.ds(m, 16, stride=16), :] for m in range(16)]
            + [jnp.zeros((16, 384), jnp.float32)],
            axis=1,
        )
        for shift in range(4):
            band[half, shift * 16 : shift * 16 + 16, :] = pltpu.roll(
                wide, 128 + 32 * shift, 1
            ).astype(jnp.bfloat16)
    place = ((y + 4 - offset) % 4) * 2
    even_rows, odd_rows, sides = [], [], []
    for group in range(5):
        sides += [
            padded[place + half, 64 - 16 * group : 576 - 16 * group, :] for half in range(2)
        ]
        for rows, step in ((even_rows, 2 * group), (odd_rows, 2 * group + 1)):
            if step <= 8:
                for half in range(2):
                    for late in range(2):
                        first = (2 * step - late + 1) * 128
                        rows.append(band[half, :, first : first + 256])
    even = jnp.dot(
        jnp.concatenate(sides, axis=1),
        jnp.concatenate(even_rows, axis=0),
        preferred_element_type=jnp.float32,
    )
    odd = jnp.dot(
        jnp.concatenate(sides[:8], axis=1),
        jnp.concatenate(odd_rows, axis=0),
        preferred_element_type=jnp.float32,
    )
    if so_far is None:
        total[:8, :] = even[:8, :]
        total[8:, :] = even[8:, :] + odd[:504, :]
    else:
        total[:8, :] = so_far[:8, :] + even[:8, :]
        total[8:, :] = so_far[8:, :] + even[8:, :] + odd[:504, :]


def first_kernel(own, padded, total, band, rows):
    add_products(0, own, padded, band, rows, None, total)


def middle_kernel(offset, response, padded, so_far, total, band, rows):
    add_products(offset, response, padded, band, rows, so_far, total)


def last_kernel(before, padded, so_far, out, band, rows, total, placed):
    add_products(1, before, padded, band, rows, so_far, total)
    turned = total[...].astype(jnp.bfloat16).T
    turned = turned.astype(jnp.bfloat16)
    skewed = [pltpu.roll(turned[u * 32 : u * 32 + 32, :], u, 1) for u in range(8)]
    lane = lax.broadcasted_iota(jnp.int32, (32, 512), 1)
    for r in range(8):
        mixed = skewed[0]
        for u in range(1, 8):
            mixed = jnp.where(lane % 8 == (r + u) % 8, skewed[u], mixed)
        mixed = pltpu.roll(mixed, (512 - r) % 512, 1)
        for part in range(4):
            placed[part, pl.ds(r, 32, stride=8), :] = mixed[:, part * 128 : part * 128 + 128].astype(jnp.float32)
    for part in range(4):
        out[:, :, part * 128 : part * 128 + 128] = placed[part].reshape(32, 8, 128).astype(jnp.bfloat16)


def call(body, shape, dtype, operands, scratch, flops=0):
    return pl.pallas_call(
        body,
        out_shape=jax.ShapeDtypeStruct(shape, dtype),
        in_specs=[VMEM] * len(operands),
        out_specs=VMEM,
        scratch_shapes=[pltpu.VMEM(s, d) for s, d in scratch],
        compiler_params=PARAMS,
        cost_estimate=pl.CostEstimate(flops=flops, bytes_accessed=2**20, transcendentals=0),
    )(*operands)


def shards(response, traces):
    f32, bf16 = jnp.float32, jnp.bfloat16
    band = [((2, 64, 19 * 128), bf16), ((2, 256, 128), f32)]

    def along_z(step):
        return lambda i: (i // 8) * 8 + step(i % 8) % 8

    def along_y(offset):
        return lambda i: (i // 8 + offset) % 4 * 8 + i % 8

    def along_x(i):
        return ((i // 2 + sign(i)) % 4) * 2 + i % 2

    def across_x(i):
        return (i + 4) % 8

    def swap(value):
        return spread(value, "shot", lambda i: i ^ 1)

    response = response.reshape(128, 64)
    held = call(
        prepare_responses,
        (2, 64, 128),
        bf16,
        (spread(response, "shot", lambda i: i), spread(response, "rcv", along_z(lambda z: z + sign(z)))),
        [((2, 128, 128), f32), ((2, 64, 128), f32)],
        JOIN_COST,
    )
    both = call(
        prepare_traces,
        (2, 512, 128),
        bf16,
        (spread(traces, "shot", lambda i: i), swap(traces)),
        [((2, 4, 128, 128), f32), ((2, 512, 128), f32)],
    )
    arrived = [
        spread(held, "rcv", along_z(lambda z, hops=hops: z - hops * sign(z))) for hops in (3, 2, 1)
    ]
    held = call(join, (8, 64, 128), bf16, (held, *arrived), [], JOIN_COST)
    before, after, across = [spread(held, "rcv", along_y(offset)) for offset in (1, 3, 2)]

    near = spread(both, "shot", along_x)
    far = spread(both, "shot", across_x)
    pieces = (both, near, swap(near), far)
    padded = call(assemble, (8, 576, 128), bf16, pieces, [])
    work = 2 * 512 * 256 * 9 * 256
    total = call(first_kernel, (512, 256), f32, (held, padded), band, work)
    for offset, block in ((2, across), (3, after)):
        body = functools.partial(middle_kernel, offset)
        total = call(body, (512, 256), f32, (block, padded, total), band, work)
    return call(
        last_kernel,
        (32, 8, 512),
        bf16,
        (before, padded, total),
        band + [((512, 256), f32), ((4, 256, 128), f32)],
        work,
    )


def solution(mesh):
    placed = (P("shot", "rcv", None), P("shot", "rcv", None))
    return jax.shard_map(
        shards, mesh=mesh, in_specs=placed, out_specs=P("shot", "rcv", None), check_vma=False
    )
```

```python
import functools

import jax
import jax.numpy as jnp
from jax import lax
from jax.experimental import pallas as pl
from jax.experimental.pallas import tpu as pltpu
from jax.sharding import PartitionSpec as P

RING8 = (0, 1, 5, 4, 2, 3, 7, 6)
VMEM = pl.BlockSpec(memory_space=pltpu.VMEM)
JOIN_COST = 2**33
PARAMS = pltpu.CompilerParams(vmem_limit_bytes=40 * 2**20)


def spread(value, axis, partner):
    size = lax.axis_size(axis)
    return lax.ppermute(value, axis, [(i, partner(i)) for i in range(size)])


def sign(coordinate):
    return 1 - 2 * (coordinate % 2)


def prepare_response(response, out, rows, turned):
    wide = response[...].astype(jnp.float32)
    rows[...] = jnp.concatenate([wide, jnp.zeros((128, 64), jnp.float32)], axis=1)
    by_position = jnp.concatenate([rows[pl.ds(k, 32, stride=4), :] for k in range(4)], axis=0)
    turned[...] = by_position.T[:64, :]
    skewed = [pltpu.roll(turned[pl.ds(u, 16, stride=4), :], 32 * u, 1) for u in range(4)]
    lane_block = lax.broadcasted_iota(jnp.int32, (16, 128), 1) // 32
    for k in range(4):
        mixed = skewed[0]
        for u in range(1, 4):
            mixed = jnp.where(lane_block == (k + u) % 4, skewed[u], mixed)
        out[k * 16 : k * 16 + 16, :] = pltpu.roll(mixed, (128 - 32 * k) % 128, 1).astype(jnp.bfloat16)


def prepare_traces(own, other, _, out, rows, turned):
    lane_block = lax.broadcasted_iota(jnp.int32, (64, 128), 1) // 16
    for side, traces in enumerate((own, other)):
        for part in range(4):
            lanes = traces[:, :, part * 128 : part * 128 + 128]
            rows[side, part] = lanes.astype(jnp.float32).reshape(128, 128)
        for part in range(4):
            by_receiver = [rows[side, part, pl.ds(r, 16, stride=8), :] for r in range(8)]
            turned[side, part * 128 : part * 128 + 128, :] = jnp.concatenate(by_receiver, axis=0).T
        skewed = [pltpu.roll(turned[side, pl.ds(d, 64, stride=8), :], 16 * d, 1) for d in range(8)]
        for r in range(8):
            mixed = skewed[0]
            for d in range(1, 8):
                mixed = jnp.where(lane_block == (r + d) % 8, skewed[d], mixed)
            turned[side, pl.ds(r, 64, stride=8), :] = pltpu.roll(mixed, (128 - 16 * r) % 128, 1)
        out[side] = turned[side].astype(jnp.bfloat16)


def assemble(own, near, near_swapped, far, out):
    shot = lax.axis_index("shot")
    x, core = shot // 2, shot % 2
    back = 4 - sign(core)
    blocks = (
        (own.at[0], x, core),
        (own.at[1], x, 1 - core),
        (near.at[0], x + back, core),
        (near.at[1], x + back, 1 - core),
        (near_swapped.at[0], x + 8 - back, 1 - core),
        (near_swapped.at[1], x + 8 - back, core),
        (far.at[0], x + 2, core),
        (far.at[1], x + 2, 1 - core),
    )
    for block, chip, side in blocks:
        place = (chip % 4) * 2 + side
        out[place, :64, :] = jnp.zeros((64, 128), jnp.bfloat16)
        out[place, 64:, :] = block[...]


def join(*blocks):
    out = blocks[-1]
    count = blocks[0].shape[0]
    for place, block in enumerate(blocks[:-1]):
        out[place * count : place * count + count] = block[...]


def position_of(offset):
    slot = jnp.int32(0)
    for index in range(1, 8):
        slot = jnp.where(offset == RING8[index], index, slot)
    return slot


def add_products(offset, response, padded, band, rows_f32, so_far, total):
    rcv = lax.axis_index("rcv")
    y, z = rcv // 8, rcv % 8
    slots = [position_of((sign(z) * (wanted - z) + 64) % 8) for wanted in range(8)]
    for half in range(2):
        for q in range(4):
            piece = response[slots[half * 4 + q]]
            rows_f32[half, q * 64 : q * 64 + 64, :] = piece.astype(jnp.float32)
        wide = jnp.concatenate(
            [rows_f32[half, pl.ds(m, 16, stride=16), :] for m in range(16)]
            + [jnp.zeros((16, 384), jnp.float32)],
            axis=1,
        )
        for shift in range(4):
            band[half, shift * 16 : shift * 16 + 16, :] = pltpu.roll(
                wide, 128 + 32 * shift, 1
            ).astype(jnp.bfloat16)
    place = ((y + 4 - offset) % 4) * 2
    even_rows, odd_rows, sides = [], [], []
    for group in range(5):
        sides += [
            padded[place + half, 64 - 16 * group : 576 - 16 * group, :] for half in range(2)
        ]
        for rows, step in ((even_rows, 2 * group), (odd_rows, 2 * group + 1)):
            if step <= 8:
                for half in range(2):
                    for late in range(2):
                        first = (2 * step - late + 1) * 128
                        rows.append(band[half, :, first : first + 256])
    even = jnp.dot(
        jnp.concatenate(sides, axis=1),
        jnp.concatenate(even_rows, axis=0),
        preferred_element_type=jnp.float32,
    )
    odd = jnp.dot(
        jnp.concatenate(sides[:8], axis=1),
        jnp.concatenate(odd_rows, axis=0),
        preferred_element_type=jnp.float32,
    )
    if so_far is None:
        total[:8, :] = even[:8, :]
        total[8:, :] = even[8:, :] + odd[:504, :]
    else:
        total[:8, :] = so_far[:8, :] + even[:8, :]
        total[8:, :] = so_far[8:, :] + even[8:, :] + odd[:504, :]


def first_kernel(own, padded, total, band, rows):
    add_products(0, own, padded, band, rows, None, total)


def middle_kernel(offset, response, padded, so_far, total, band, rows):
    add_products(offset, response, padded, band, rows, so_far, total)


def last_kernel(before, padded, so_far, out, band, rows, total, placed):
    add_products(1, before, padded, band, rows, so_far, total)
    turned = total[...].astype(jnp.bfloat16).T
    turned = turned.astype(jnp.bfloat16)
    skewed = [pltpu.roll(turned[u * 32 : u * 32 + 32, :], u, 1) for u in range(8)]
    lane = lax.broadcasted_iota(jnp.int32, (32, 512), 1)
    for r in range(8):
        mixed = skewed[0]
        for u in range(1, 8):
            mixed = jnp.where(lane % 8 == (r + u) % 8, skewed[u], mixed)
        mixed = pltpu.roll(mixed, (512 - r) % 512, 1)
        for part in range(4):
            placed[part, pl.ds(r, 32, stride=8), :] = mixed[:, part * 128 : part * 128 + 128].astype(jnp.float32)
    for part in range(4):
        out[:, :, part * 128 : part * 128 + 128] = placed[part].reshape(32, 8, 128).astype(jnp.bfloat16)


def call(body, shape, dtype, operands, scratch, flops=0):
    return pl.pallas_call(
        body,
        out_shape=jax.ShapeDtypeStruct(shape, dtype),
        in_specs=[VMEM] * len(operands),
        out_specs=VMEM,
        scratch_shapes=[pltpu.VMEM(s, d) for s, d in scratch],
        compiler_params=PARAMS,
        cost_estimate=pl.CostEstimate(flops=flops, bytes_accessed=2**20, transcendentals=0),
    )(*operands)


def shards(response, traces):
    f32, bf16 = jnp.float32, jnp.bfloat16
    band = [((2, 64, 19 * 128), bf16), ((2, 256, 128), f32)]

    def along_z(step):
        return lambda i: (i // 8) * 8 + step(i % 8) % 8

    def along_y(offset):
        return lambda i: (i // 8 + offset) % 4 * 8 + i % 8

    def along_x(i):
        return ((i // 2 + sign(i)) % 4) * 2 + i % 2

    def across_x(i):
        return (i + 4) % 8

    def swap(value):
        return spread(value, "shot", lambda i: i ^ 1)

    held = call(
        prepare_response,
        (64, 128),
        bf16,
        (response.reshape(128, 64),),
        [((128, 128), f32), ((64, 128), f32)],
    )
    held = held[None]
    both = call(
        prepare_traces,
        (2, 512, 128),
        bf16,
        (traces, swap(traces), held),
        [((2, 4, 128, 128), f32), ((2, 512, 128), f32)],
    )
    held = call(join, (2, 64, 128), bf16, (held, spread(held, "rcv", along_z(lambda z: z + sign(z)))), [], JOIN_COST)
    arrived = [
        spread(held, "rcv", along_z(lambda z, hops=hops: z - hops * sign(z))) for hops in (3, 2, 1)
    ]
    held = call(join, (8, 64, 128), bf16, (held, *arrived), [], JOIN_COST)
    before, after, across = [spread(held, "rcv", along_y(offset)) for offset in (1, 3, 2)]

    near = spread(both, "shot", along_x)
    far = spread(both, "shot", across_x)
    pieces = (both, near, swap(near), far)
    padded = call(assemble, (8, 576, 128), bf16, pieces, [])
    work = 2 * 512 * 256 * 9 * 256
    total = call(first_kernel, (512, 256), f32, (held, padded), band, work)
    for offset, block in ((2, across), (3, after)):
        body = functools.partial(middle_kernel, offset)
        total = call(body, (512, 256), f32, (block, padded, total), band, work)
    return call(
        last_kernel,
        (32, 8, 512),
        bf16,
        (before, padded, total),
        band + [((512, 256), f32), ((4, 256, 128), f32)],
        work,
    )


def solution(mesh):
    placed = (P("shot", "rcv", None), P("shot", "rcv", None))
    return jax.shard_map(
        shards, mesh=mesh, in_specs=placed, out_specs=P("shot", "rcv", None), check_vma=False
    )
```

```python
import functools

import jax
import jax.numpy as jnp
from jax import lax
from jax.experimental import pallas as pl
from jax.experimental.pallas import tpu as pltpu
from jax.sharding import PartitionSpec as P

RING8 = (0, 1, 5, 4, 2, 3, 7, 6)
VMEM = pl.BlockSpec(memory_space=pltpu.VMEM)
JOIN_COST = 2**33
PARAMS = pltpu.CompilerParams(vmem_limit_bytes=40 * 2**20)


def spread(value, axis, partner):
    size = lax.axis_size(axis)
    return lax.ppermute(value, axis, [(i, partner(i)) for i in range(size)])


def sign(coordinate):
    return 1 - 2 * (coordinate % 2)


def prepare_response(response, out, rows, turned):
    wide = response[...].astype(jnp.float32)
    rows[...] = jnp.concatenate([wide, jnp.zeros((128, 64), jnp.float32)], axis=1)
    by_position = jnp.concatenate([rows[pl.ds(k, 32, stride=4), :] for k in range(4)], axis=0)
    turned[...] = by_position.T[:64, :]
    skewed = [pltpu.roll(turned[pl.ds(u, 16, stride=4), :], 32 * u, 1) for u in range(4)]
    lane_block = lax.broadcasted_iota(jnp.int32, (16, 128), 1) // 32
    for k in range(4):
        mixed = skewed[0]
        for u in range(1, 4):
            mixed = jnp.where(lane_block == (k + u) % 4, skewed[u], mixed)
        out[k * 16 : k * 16 + 16, :] = pltpu.roll(mixed, (128 - 32 * k) % 128, 1).astype(jnp.bfloat16)


def prepare_traces(own, other, _, out, rows, turned):
    lane_block = lax.broadcasted_iota(jnp.int32, (64, 128), 1) // 16
    for side, traces in enumerate((own, other)):
        for part in range(4):
            lanes = traces[:, :, part * 128 : part * 128 + 128]
            rows[side, part] = lanes.astype(jnp.float32).reshape(128, 128)
        for part in range(4):
            by_receiver = [rows[side, part, pl.ds(r, 16, stride=8), :] for r in range(8)]
            turned[side, part * 128 : part * 128 + 128, :] = jnp.concatenate(by_receiver, axis=0).T
        skewed = [
            pltpu.roll(turned[side, pl.ds(d, 64, stride=8), :].astype(jnp.bfloat16), 16 * d, 1)
            for d in range(8)
        ]
        for r in range(8):
            mixed = skewed[0]
            for d in range(1, 8):
                mixed = jnp.where(lane_block == (r + d) % 8, skewed[d], mixed)
            mixed = pltpu.roll(mixed, (128 - 16 * r) % 128, 1)
            turned[side, pl.ds(r, 64, stride=8), :] = mixed.astype(jnp.float32)
        out[side] = turned[side].astype(jnp.bfloat16)


def assemble(own, near, near_swapped, far, out):
    shot = lax.axis_index("shot")
    x, core = shot // 2, shot % 2
    back = 4 - sign(core)
    blocks = (
        (own.at[0], x, core),
        (own.at[1], x, 1 - core),
        (near.at[0], x + back, core),
        (near.at[1], x + back, 1 - core),
        (near_swapped.at[0], x + 8 - back, 1 - core),
        (near_swapped.at[1], x + 8 - back, core),
        (far.at[0], x + 2, core),
        (far.at[1], x + 2, 1 - core),
    )
    for block, chip, side in blocks:
        place = (chip % 4) * 2 + side
        out[place, :64, :] = jnp.zeros((64, 128), jnp.bfloat16)
        out[place, 64:, :] = block[...]


def join(*blocks):
    out = blocks[-1]
    count = blocks[0].shape[0]
    for place, block in enumerate(blocks[:-1]):
        out[place * count : place * count + count] = block[...]


def position_of(offset):
    slot = jnp.int32(0)
    for index in range(1, 8):
        slot = jnp.where(offset == RING8[index], index, slot)
    return slot


def add_products(offset, response, padded, band, rows_f32, so_far, total):
    rcv = lax.axis_index("rcv")
    y, z = rcv // 8, rcv % 8
    slots = [position_of((sign(z) * (wanted - z) + 64) % 8) for wanted in range(8)]
    for half in range(2):
        for q in range(4):
            piece = response[slots[half * 4 + q]]
            rows_f32[half, q * 64 : q * 64 + 64, :] = piece.astype(jnp.float32)
        wide = jnp.concatenate(
            [rows_f32[half, pl.ds(m, 16, stride=16), :] for m in range(16)]
            + [jnp.zeros((16, 384), jnp.float32)],
            axis=1,
        )
        for shift in range(4):
            band[half, shift * 16 : shift * 16 + 16, :] = pltpu.roll(
                wide, 128 + 32 * shift, 1
            ).astype(jnp.bfloat16)
    place = ((y + 4 - offset) % 4) * 2
    even_rows, odd_rows, sides = [], [], []
    for group in range(5):
        sides += [
            padded[place + half, 64 - 16 * group : 576 - 16 * group, :] for half in range(2)
        ]
        for rows, step in ((even_rows, 2 * group), (odd_rows, 2 * group + 1)):
            if step <= 8:
                for half in range(2):
                    for late in range(2):
                        first = (2 * step - late + 1) * 128
                        rows.append(band[half, :, first : first + 256])
    even = jnp.dot(
        jnp.concatenate(sides, axis=1),
        jnp.concatenate(even_rows, axis=0),
        preferred_element_type=jnp.float32,
    )
    odd = jnp.dot(
        jnp.concatenate(sides[:8], axis=1),
        jnp.concatenate(odd_rows, axis=0),
        preferred_element_type=jnp.float32,
    )
    if so_far is None:
        total[:8, :] = even[:8, :]
        total[8:, :] = even[8:, :] + odd[:504, :]
    else:
        total[:8, :] = so_far[:8, :] + even[:8, :]
        total[8:, :] = so_far[8:, :] + even[8:, :] + odd[:504, :]


def first_kernel(own, padded, total, band, rows):
    add_products(0, own, padded, band, rows, None, total)


def middle_kernel(offset, response, padded, so_far, total, band, rows):
    add_products(offset, response, padded, band, rows, so_far, total)


def last_kernel(after, padded, so_far, out, band, rows, total, placed):
    add_products(3, after, padded, band, rows, so_far, total)
    turned = total[...].astype(jnp.bfloat16).T
    turned = turned.astype(jnp.bfloat16)
    skewed = [pltpu.roll(turned[u * 32 : u * 32 + 32, :], u, 1) for u in range(8)]
    lane = lax.broadcasted_iota(jnp.int32, (32, 512), 1)
    for r in range(8):
        mixed = skewed[0]
        for u in range(1, 8):
            mixed = jnp.where(lane % 8 == (r + u) % 8, skewed[u], mixed)
        mixed = pltpu.roll(mixed, (512 - r) % 512, 1)
        for part in range(4):
            placed[part, pl.ds(r, 32, stride=8), :] = mixed[:, part * 128 : part * 128 + 128].astype(jnp.float32)
    for part in range(4):
        out[:, :, part * 128 : part * 128 + 128] = placed[part].reshape(32, 8, 128).astype(jnp.bfloat16)


def call(body, shape, dtype, operands, scratch, flops=0):
    return pl.pallas_call(
        body,
        out_shape=jax.ShapeDtypeStruct(shape, dtype),
        in_specs=[VMEM] * len(operands),
        out_specs=VMEM,
        scratch_shapes=[pltpu.VMEM(s, d) for s, d in scratch],
        compiler_params=PARAMS,
        cost_estimate=pl.CostEstimate(flops=flops, bytes_accessed=2**20, transcendentals=0),
    )(*operands)


def shards(response, traces):
    f32, bf16 = jnp.float32, jnp.bfloat16
    band = [((2, 64, 19 * 128), bf16), ((2, 256, 128), f32)]

    def along_z(step):
        return lambda i: (i // 8) * 8 + step(i % 8) % 8

    def along_y(offset):
        return lambda i: (i // 8 + offset) % 4 * 8 + i % 8

    def along_x(i):
        return ((i // 2 + sign(i)) % 4) * 2 + i % 2

    def across_x(i):
        return (i + 4) % 8

    def swap(value):
        return spread(value, "shot", lambda i: i ^ 1)

    held = call(
        prepare_response,
        (64, 128),
        bf16,
        (response.reshape(128, 64),),
        [((128, 128), f32), ((64, 128), f32)],
    )
    held = held[None]
    both = call(
        prepare_traces,
        (2, 512, 128),
        bf16,
        (traces, swap(traces), held),
        [((2, 4, 128, 128), f32), ((2, 512, 128), f32)],
    )
    held = call(join, (2, 64, 128), bf16, (held, spread(held, "rcv", along_z(lambda z: z + sign(z)))), [], JOIN_COST)
    arrived = [
        spread(held, "rcv", along_z(lambda z, hops=hops: z - hops * sign(z))) for hops in (3, 2, 1)
    ]
    held = call(join, (8, 64, 128), bf16, (held, *arrived), [], JOIN_COST)
    before, after, across = [spread(held, "rcv", along_y(offset)) for offset in (1, 3, 2)]

    near = spread(both, "shot", along_x)
    far = spread(both, "shot", across_x)
    pieces = (both, near, swap(near), far)
    padded = call(assemble, (8, 576, 128), bf16, pieces, [])
    work = 2 * 512 * 256 * 9 * 256
    total = call(first_kernel, (512, 256), f32, (held, padded), band, work)
    for offset, block in ((2, across), (1, before)):
        body = functools.partial(middle_kernel, offset)
        total = call(body, (512, 256), f32, (block, padded, total), band, work)
    return call(
        last_kernel,
        (32, 8, 512),
        bf16,
        (after, padded, total),
        band + [((512, 256), f32), ((4, 256, 128), f32)],
        work,
    )


def solution(mesh):
    placed = (P("shot", "rcv", None), P("shot", "rcv", None))
    return jax.shard_map(
        shards, mesh=mesh, in_specs=placed, out_specs=P("shot", "rcv", None), check_vma=False
    )
```

```python
import functools

import jax
import jax.numpy as jnp
from jax import lax
from jax.experimental import pallas as pl
from jax.experimental.pallas import tpu as pltpu
from jax.sharding import PartitionSpec as P

RING8 = (0, 1, 5, 4, 2, 3, 7, 6)
VMEM = pl.BlockSpec(memory_space=pltpu.VMEM)
JOIN_COST = 2**33
PARAMS = pltpu.CompilerParams(vmem_limit_bytes=40 * 2**20)


def spread(value, axis, partner):
    size = lax.axis_size(axis)
    return lax.ppermute(value, axis, [(i, partner(i)) for i in range(size)])


def sign(coordinate):
    return 1 - 2 * (coordinate % 2)


def prepare_responses(own, neighbour, out, rows, turned):
    lane_block = lax.broadcasted_iota(jnp.int32, (16, 128), 1) // 32
    for side, response in enumerate((own, neighbour)):
        wide = response[...].astype(jnp.float32)
        rows[side] = jnp.concatenate([wide, jnp.zeros((128, 64), jnp.float32)], axis=1)
        by_position = [rows[side, pl.ds(k, 32, stride=4), :] for k in range(4)]
        turned[side] = jnp.concatenate(by_position, axis=0).T[:64, :]
        skewed = [pltpu.roll(turned[side, pl.ds(u, 16, stride=4), :], 32 * u, 1) for u in range(4)]
        for k in range(4):
            mixed = skewed[0]
            for u in range(1, 4):
                mixed = jnp.where(lane_block == (k + u) % 4, skewed[u], mixed)
            mixed = pltpu.roll(mixed, (128 - 32 * k) % 128, 1)
            out[side, k * 16 : k * 16 + 16, :] = mixed.astype(jnp.bfloat16)


def prepare_traces(own, other, out, rows, turned):
    lane_block = lax.broadcasted_iota(jnp.int32, (64, 128), 1) // 16
    for side, traces in enumerate((own, other)):
        for part in range(4):
            lanes = traces[:, :, part * 128 : part * 128 + 128]
            rows[side, part] = lanes.astype(jnp.float32).reshape(128, 128)
        for part in range(4):
            by_receiver = [rows[side, part, pl.ds(r, 16, stride=8), :] for r in range(8)]
            turned[side, part * 128 : part * 128 + 128, :] = jnp.concatenate(by_receiver, axis=0).T
        skewed = [
            pltpu.roll(turned[side, pl.ds(d, 64, stride=8), :].astype(jnp.bfloat16), 16 * d, 1)
            for d in range(8)
        ]
        for r in range(8):
            mixed = skewed[0]
            for d in range(1, 8):
                mixed = jnp.where(lane_block == (r + d) % 8, skewed[d], mixed)
            mixed = pltpu.roll(mixed, (128 - 16 * r) % 128, 1)
            turned[side, pl.ds(r, 64, stride=8), :] = mixed.astype(jnp.float32)
        out[side] = turned[side].astype(jnp.bfloat16)


def assemble(own, near, near_swapped, far, out):
    shot = lax.axis_index("shot")
    x, core = shot // 2, shot % 2
    back = 4 - sign(core)
    blocks = (
        (own.at[0], x, core),
        (own.at[1], x, 1 - core),
        (near.at[0], x + back, core),
        (near.at[1], x + back, 1 - core),
        (near_swapped.at[0], x + 8 - back, 1 - core),
        (near_swapped.at[1], x + 8 - back, core),
        (far.at[0], x + 2, core),
        (far.at[1], x + 2, 1 - core),
    )
    for block, chip, side in blocks:
        place = (chip % 4) * 2 + side
        out[place, :64, :] = jnp.zeros((64, 128), jnp.bfloat16)
        out[place, 64:, :] = block[...]


def join(*blocks):
    out = blocks[-1]
    count = blocks[0].shape[0]
    for place, block in enumerate(blocks[:-1]):
        out[place * count : place * count + count] = block[...]


def position_of(offset):
    slot = jnp.int32(0)
    for index in range(1, 8):
        slot = jnp.where(offset == RING8[index], index, slot)
    return slot


def add_products(offset, response, padded, band, rows_f32, so_far, total):
    rcv = lax.axis_index("rcv")
    y, z = rcv // 8, rcv % 8
    slots = [position_of((sign(z) * (wanted - z) + 64) % 8) for wanted in range(8)]
    for half in range(2):
        for q in range(4):
            piece = response[slots[half * 4 + q]]
            rows_f32[half, q * 64 : q * 64 + 64, :] = piece.astype(jnp.float32)
        wide = jnp.concatenate(
            [rows_f32[half, pl.ds(m, 16, stride=16), :] for m in range(16)]
            + [jnp.zeros((16, 384), jnp.float32)],
            axis=1,
        )
        for shift in range(4):
            band[half, shift * 16 : shift * 16 + 16, :] = pltpu.roll(
                wide, 128 + 32 * shift, 1
            ).astype(jnp.bfloat16)
    place = ((y + 4 - offset) % 4) * 2
    even_rows, odd_rows, sides = [], [], []
    for group in range(5):
        sides += [
            padded[place + half, 64 - 16 * group : 576 - 16 * group, :] for half in range(2)
        ]
        for rows, step in ((even_rows, 2 * group), (odd_rows, 2 * group + 1)):
            if step <= 8:
                for half in range(2):
                    for late in range(2):
                        first = (2 * step - late + 1) * 128
                        rows.append(band[half, :, first : first + 256])
    even = jnp.dot(
        jnp.concatenate(sides, axis=1),
        jnp.concatenate(even_rows, axis=0),
        preferred_element_type=jnp.float32,
    )
    odd = jnp.dot(
        jnp.concatenate(sides[:8], axis=1),
        jnp.concatenate(odd_rows, axis=0),
        preferred_element_type=jnp.float32,
    )
    if so_far is None:
        total[:8, :] = even[:8, :]
        total[8:, :] = even[8:, :] + odd[:504, :]
    else:
        total[:8, :] = so_far[:8, :] + even[:8, :]
        total[8:, :] = so_far[8:, :] + even[8:, :] + odd[:504, :]


def first_kernel(own, padded, total, band, rows):
    add_products(0, own, padded, band, rows, None, total)


def middle_kernel(offset, response, padded, so_far, total, band, rows):
    add_products(offset, response, padded, band, rows, so_far, total)


def last_kernel(before, padded, so_far, out, band, rows, total, placed):
    add_products(1, before, padded, band, rows, so_far, total)
    turned = total[...].astype(jnp.bfloat16).T
    turned = turned.astype(jnp.bfloat16)
    skewed = [pltpu.roll(turned[u * 32 : u * 32 + 32, :], u, 1) for u in range(8)]
    lane = lax.broadcasted_iota(jnp.int32, (32, 512), 1)
    for r in range(8):
        mixed = skewed[0]
        for u in range(1, 8):
            mixed = jnp.where(lane % 8 == (r + u) % 8, skewed[u], mixed)
        mixed = pltpu.roll(mixed, (512 - r) % 512, 1)
        for part in range(4):
            placed[part, pl.ds(r, 32, stride=8), :] = mixed[:, part * 128 : part * 128 + 128].astype(jnp.float32)
    for part in range(4):
        out[:, :, part * 128 : part * 128 + 128] = placed[part].reshape(32, 8, 128).astype(jnp.bfloat16)


def call(body, shape, dtype, operands, scratch, flops=0):
    return pl.pallas_call(
        body,
        out_shape=jax.ShapeDtypeStruct(shape, dtype),
        in_specs=[VMEM] * len(operands),
        out_specs=VMEM,
        scratch_shapes=[pltpu.VMEM(s, d) for s, d in scratch],
        compiler_params=PARAMS,
        cost_estimate=pl.CostEstimate(flops=flops, bytes_accessed=2**20, transcendentals=0),
    )(*operands)


def shards(response, traces):
    f32, bf16 = jnp.float32, jnp.bfloat16
    band = [((2, 64, 19 * 128), bf16), ((2, 256, 128), f32)]

    def along_z(step):
        return lambda i: (i // 8) * 8 + step(i % 8) % 8

    def along_y(offset):
        return lambda i: (i // 8 + offset) % 4 * 8 + i % 8

    def along_x(i):
        return ((i // 2 + sign(i)) % 4) * 2 + i % 2

    def across_x(i):
        return (i + 4) % 8

    def swap(value):
        return spread(value, "shot", lambda i: i ^ 1)

    response = response.reshape(128, 64)
    held = call(
        prepare_responses,
        (2, 64, 128),
        bf16,
        (response, spread(response, "rcv", along_z(lambda z: z + sign(z)))),
        [((2, 128, 128), f32), ((2, 64, 128), f32)],
        JOIN_COST,
    )
    both = call(
        prepare_traces,
        (2, 512, 128),
        bf16,
        (traces, swap(traces)),
        [((2, 4, 128, 128), f32), ((2, 512, 128), f32)],
    )
    arrived = [
        spread(held, "rcv", along_z(lambda z, hops=hops: z - hops * sign(z))) for hops in (3, 2, 1)
    ]
    held = call(join, (8, 64, 128), bf16, (held, *arrived), [], JOIN_COST)
    before, after, across = [spread(held, "rcv", along_y(offset)) for offset in (1, 3, 2)]

    near = spread(both, "shot", along_x)
    far = spread(both, "shot", across_x)
    pieces = (both, near, swap(near), far)
    padded = call(assemble, (8, 576, 128), bf16, pieces, [])
    work = 2 * 512 * 256 * 9 * 256
    total = call(first_kernel, (512, 256), f32, (held, padded), band, work)
    for offset, block in ((2, across), (3, after)):
        body = functools.partial(middle_kernel, offset)
        total = call(body, (512, 256), f32, (block, padded, total), band, work)
    return call(
        last_kernel,
        (32, 8, 512),
        bf16,
        (before, padded, total),
        band + [((512, 256), f32), ((4, 256, 128), f32)],
        work,
    )


def solution(mesh):
    placed = (P("shot", "rcv", None), P("shot", "rcv", None))
    return jax.shard_map(
        shards, mesh=mesh, in_specs=placed, out_specs=P("shot", "rcv", None), check_vma=False
    )
```

```python
import functools

import jax
import jax.numpy as jnp
from jax import lax
from jax.experimental import pallas as pl
from jax.experimental.pallas import tpu as pltpu
from jax.sharding import PartitionSpec as P

RING8 = (0, 1, 5, 4, 2, 3, 7, 6)
VMEM = pl.BlockSpec(memory_space=pltpu.VMEM)
JOIN_COST = 2**33
PARAMS = pltpu.CompilerParams(vmem_limit_bytes=40 * 2**20)


def spread(value, axis, partner):
    size = lax.axis_size(axis)
    return lax.ppermute(value, axis, [(i, partner(i)) for i in range(size)])


def sign(coordinate):
    return 1 - 2 * (coordinate % 2)


def prepare_response(response, out, rows, turned):
    wide = response[...].astype(jnp.float32)
    rows[...] = jnp.concatenate([wide, jnp.zeros((128, 64), jnp.float32)], axis=1)
    by_position = jnp.concatenate([rows[pl.ds(k, 32, stride=4), :] for k in range(4)], axis=0)
    turned[...] = by_position.T[:64, :]
    skewed = [pltpu.roll(turned[pl.ds(u, 16, stride=4), :], 32 * u, 1) for u in range(4)]
    lane_block = lax.broadcasted_iota(jnp.int32, (16, 128), 1) // 32
    for k in range(4):
        mixed = skewed[0]
        for u in range(1, 4):
            mixed = jnp.where(lane_block == (k + u) % 4, skewed[u], mixed)
        out[k * 16 : k * 16 + 16, :] = pltpu.roll(mixed, (128 - 32 * k) % 128, 1).astype(jnp.bfloat16)


def prepare_traces(own, other, _, out, rows, turned):
    lane_block = lax.broadcasted_iota(jnp.int32, (64, 128), 1) // 16
    for side, traces in enumerate((own, other)):
        for part in range(4):
            lanes = traces[:, :, part * 128 : part * 128 + 128]
            rows[side, part] = lanes.astype(jnp.float32).reshape(128, 128)
        for part in range(4):
            by_receiver = [rows[side, part, pl.ds(r, 16, stride=8), :] for r in range(8)]
            turned[side, part * 128 : part * 128 + 128, :] = jnp.concatenate(by_receiver, axis=0).T
        skewed = [
            pltpu.roll(turned[side, pl.ds(d, 64, stride=8), :].astype(jnp.bfloat16), 16 * d, 1)
            for d in range(8)
        ]
        for r in range(8):
            mixed = skewed[0]
            for d in range(1, 8):
                mixed = jnp.where(lane_block == (r + d) % 8, skewed[d], mixed)
            mixed = pltpu.roll(mixed, (128 - 16 * r) % 128, 1)
            turned[side, pl.ds(r, 64, stride=8), :] = mixed.astype(jnp.float32)
        out[side] = turned[side].astype(jnp.bfloat16)


def assemble(own, near, near_swapped, far, out):
    shot = lax.axis_index("shot")
    x, core = shot // 2, shot % 2
    back = 4 - sign(core)
    blocks = (
        (own.at[0], x, core),
        (own.at[1], x, 1 - core),
        (near.at[0], x + back, core),
        (near.at[1], x + back, 1 - core),
        (near_swapped.at[0], x + 8 - back, 1 - core),
        (near_swapped.at[1], x + 8 - back, core),
        (far.at[0], x + 2, core),
        (far.at[1], x + 2, 1 - core),
    )
    for block, chip, side in blocks:
        place = (chip % 4) * 2 + side
        out[place, :64, :] = jnp.zeros((64, 128), jnp.bfloat16)
        out[place, 64:, :] = block[...]


def join(*blocks):
    out = blocks[-1]
    count = blocks[0].shape[0]
    for place, block in enumerate(blocks[:-1]):
        out[place * count : place * count + count] = block[...]


def position_of(offset):
    slot = jnp.int32(0)
    for index in range(1, 8):
        slot = jnp.where(offset == RING8[index], index, slot)
    return slot


def add_products(offset, response, padded, band, rows_f32, so_far, total):
    rcv = lax.axis_index("rcv")
    y, z = rcv // 8, rcv % 8
    slots = [position_of((sign(z) * (wanted - z) + 64) % 8) for wanted in range(8)]
    for half in range(2):
        for q in range(4):
            piece = response[slots[half * 4 + q]]
            rows_f32[half, q * 64 : q * 64 + 64, :] = piece.astype(jnp.float32)
        wide = jnp.concatenate(
            [rows_f32[half, pl.ds(m, 16, stride=16), :] for m in range(16)]
            + [jnp.zeros((16, 384), jnp.float32)],
            axis=1,
        )
        for shift in range(4):
            band[half, shift * 16 : shift * 16 + 16, :] = pltpu.roll(
                wide, 128 + 32 * shift, 1
            ).astype(jnp.bfloat16)
    if offset % 2:
        offset = offset * sign(lax.axis_index("shot") % 2)
    place = ((y + 4 - offset) % 4) * 2
    even_rows, odd_rows, sides = [], [], []
    for group in range(5):
        sides += [
            padded[place + half, 64 - 16 * group : 576 - 16 * group, :] for half in range(2)
        ]
        for rows, step in ((even_rows, 2 * group), (odd_rows, 2 * group + 1)):
            if step <= 8:
                for half in range(2):
                    for late in range(2):
                        first = (2 * step - late + 1) * 128
                        rows.append(band[half, :, first : first + 256])
    even = jnp.dot(
        jnp.concatenate(sides, axis=1),
        jnp.concatenate(even_rows, axis=0),
        preferred_element_type=jnp.float32,
    )
    odd = jnp.dot(
        jnp.concatenate(sides[:8], axis=1),
        jnp.concatenate(odd_rows, axis=0),
        preferred_element_type=jnp.float32,
    )
    if so_far is None:
        total[:8, :] = even[:8, :]
        total[8:, :] = even[8:, :] + odd[:504, :]
    else:
        total[:8, :] = so_far[:8, :] + even[:8, :]
        total[8:, :] = so_far[8:, :] + even[8:, :] + odd[:504, :]


def first_kernel(own, padded, total, band, rows):
    add_products(0, own, padded, band, rows, None, total)


def middle_kernel(offset, response, padded, so_far, total, band, rows):
    add_products(offset, response, padded, band, rows, so_far, total)


def last_kernel(outward, padded, so_far, out, band, rows, total, placed):
    add_products(1, outward, padded, band, rows, so_far, total)
    turned = total[...].astype(jnp.bfloat16).T
    turned = turned.astype(jnp.bfloat16)
    skewed = [pltpu.roll(turned[u * 32 : u * 32 + 32, :], u, 1) for u in range(8)]
    lane = lax.broadcasted_iota(jnp.int32, (32, 512), 1)
    for r in range(8):
        mixed = skewed[0]
        for u in range(1, 8):
            mixed = jnp.where(lane % 8 == (r + u) % 8, skewed[u], mixed)
        mixed = pltpu.roll(mixed, (512 - r) % 512, 1)
        for part in range(4):
            placed[part, pl.ds(r, 32, stride=8), :] = mixed[:, part * 128 : part * 128 + 128].astype(jnp.float32)
    for part in range(4):
        out[:, :, part * 128 : part * 128 + 128] = placed[part].reshape(32, 8, 128).astype(jnp.bfloat16)


def call(body, shape, dtype, operands, scratch, flops=0):
    return pl.pallas_call(
        body,
        out_shape=jax.ShapeDtypeStruct(shape, dtype),
        in_specs=[VMEM] * len(operands),
        out_specs=VMEM,
        scratch_shapes=[pltpu.VMEM(s, d) for s, d in scratch],
        compiler_params=PARAMS,
        cost_estimate=pl.CostEstimate(flops=flops, bytes_accessed=2**20, transcendentals=0),
    )(*operands)


def shards(response, traces):
    f32, bf16 = jnp.float32, jnp.bfloat16
    band = [((2, 64, 19 * 128), bf16), ((2, 256, 128), f32)]

    def along_z(step):
        return lambda i: (i // 8) * 8 + step(i % 8) % 8

    def along_y(offset):
        return lambda i: (i // 8 + offset) % 4 * 8 + i % 8

    def by_core(value, way):
        pairs = []
        for i in range(lax.axis_size("shot")):
            step = along_y(way * sign(i))
            pairs += [(i * 32 + j, i * 32 + step(j)) for j in range(lax.axis_size("rcv"))]
        return lax.ppermute(value, ("shot", "rcv"), pairs)

    def along_x(i):
        return ((i // 2 + sign(i)) % 4) * 2 + i % 2

    def across_x(i):
        return (i + 4) % 8

    def swap(value):
        return spread(value, "shot", lambda i: i ^ 1)

    held = call(
        prepare_response,
        (64, 128),
        bf16,
        (response.reshape(128, 64),),
        [((128, 128), f32), ((64, 128), f32)],
    )
    held = held[None]
    both = call(
        prepare_traces,
        (2, 512, 128),
        bf16,
        (traces, swap(traces), held),
        [((2, 4, 128, 128), f32), ((2, 512, 128), f32)],
    )
    held = call(join, (2, 64, 128), bf16, (held, spread(held, "rcv", along_z(lambda z: z + sign(z)))), [], JOIN_COST)
    arrived = [
        spread(held, "rcv", along_z(lambda z, hops=hops: z - hops * sign(z))) for hops in (3, 2, 1)
    ]
    held = call(join, (8, 64, 128), bf16, (held, *arrived), [], JOIN_COST)
    across = spread(held, "rcv", along_y(2))
    outward, inward = by_core(held, 1), by_core(held, -1)

    near = spread(both, "shot", along_x)
    far = spread(both, "shot", across_x)
    pieces = (both, near, swap(near), far)
    padded = call(assemble, (8, 576, 128), bf16, pieces, [])
    work = 2 * 512 * 256 * 9 * 256
    total = call(first_kernel, (512, 256), f32, (held, padded), band, work)
    for offset, block in ((2, across), (-1, inward)):
        body = functools.partial(middle_kernel, offset)
        total = call(body, (512, 256), f32, (block, padded, total), band, work)
    return call(
        last_kernel,
        (32, 8, 512),
        bf16,
        (outward, padded, total),
        band + [((512, 256), f32), ((4, 256, 128), f32)],
        work,
    )


def solution(mesh):
    placed = (P("shot", "rcv", None), P("shot", "rcv", None))
    return jax.shard_map(
        shards, mesh=mesh, in_specs=placed, out_specs=P("shot", "rcv", None), check_vma=False
    )
```

```python
import functools

import jax
import jax.numpy as jnp
from jax import lax
from jax.experimental import pallas as pl
from jax.experimental.pallas import tpu as pltpu
from jax.sharding import PartitionSpec as P

RING8 = (0, 1, 5, 4, 2, 3, 7, 6)
VMEM = pl.BlockSpec(memory_space=pltpu.VMEM)
JOIN_COST = 2**33
PARAMS = pltpu.CompilerParams(vmem_limit_bytes=40 * 2**20)


def spread(value, axis, partner):
    size = lax.axis_size(axis)
    return lax.ppermute(value, axis, [(i, partner(i)) for i in range(size)])


def sign(coordinate):
    return 1 - 2 * (coordinate % 2)


def prepare_response(response, out, rows, turned):
    wide = response[...].astype(jnp.float32)
    rows[...] = jnp.concatenate([wide, jnp.zeros((128, 64), jnp.float32)], axis=1)
    by_position = jnp.concatenate([rows[pl.ds(k, 32, stride=4), :] for k in range(4)], axis=0)
    turned[...] = by_position.T[:64, :]
    skewed = [pltpu.roll(turned[pl.ds(u, 16, stride=4), :], 32 * u, 1) for u in range(4)]
    lane_block = lax.broadcasted_iota(jnp.int32, (16, 128), 1) // 32
    for k in range(4):
        mixed = skewed[0]
        for u in range(1, 4):
            mixed = jnp.where(lane_block == (k + u) % 4, skewed[u], mixed)
        out[k * 16 : k * 16 + 16, :] = pltpu.roll(mixed, (128 - 32 * k) % 128, 1).astype(jnp.bfloat16)


def prepare_traces(own, other, _, out, rows, turned):
    lane_block = lax.broadcasted_iota(jnp.int32, (64, 128), 1) // 16
    for side, traces in enumerate((own, other)):
        for part in range(4):
            lanes = traces[:, :, part * 128 : part * 128 + 128]
            rows[side, part] = lanes.astype(jnp.float32).reshape(128, 128)
        for part in range(4):
            by_receiver = [rows[side, part, pl.ds(r, 16, stride=8), :] for r in range(8)]
            turned[side, part * 128 : part * 128 + 128, :] = jnp.concatenate(by_receiver, axis=0).T
        skewed = [
            pltpu.roll(turned[side, pl.ds(d, 64, stride=8), :].astype(jnp.bfloat16), 16 * d, 1)
            for d in range(8)
        ]
        for r in range(8):
            mixed = skewed[0]
            for d in range(1, 8):
                mixed = jnp.where(lane_block == (r + d) % 8, skewed[d], mixed)
            mixed = pltpu.roll(mixed, (128 - 16 * r) % 128, 1)
            turned[side, pl.ds(r, 64, stride=8), :] = mixed.astype(jnp.float32)
        out[side] = turned[side].astype(jnp.bfloat16)


def assemble(own, near, near_swapped, far, out):
    shot = lax.axis_index("shot")
    x, core = shot // 2, shot % 2
    back = 4 - sign(core)
    blocks = (
        (own.at[0], x, core),
        (own.at[1], x, 1 - core),
        (near.at[0], x + back, core),
        (near.at[1], x + back, 1 - core),
        (near_swapped.at[0], x + 8 - back, 1 - core),
        (near_swapped.at[1], x + 8 - back, core),
        (far.at[0], x + 2, core),
        (far.at[1], x + 2, 1 - core),
    )
    for block, chip, side in blocks:
        place = (chip % 4) * 2 + side
        out[place, :64, :] = jnp.zeros((64, 128), jnp.bfloat16)
        out[place, 64:, :] = block[...]


def join(*blocks):
    out = blocks[-1]
    count = blocks[0].shape[0]
    for place, block in enumerate(blocks[:-1]):
        out[place * count : place * count + count] = block[...]


def position_of(offset):
    slot = jnp.int32(0)
    for index in range(1, 8):
        slot = jnp.where(offset == RING8[index], index, slot)
    return slot


def operands(offset, response, padded, band, rows_f32):
    rcv = lax.axis_index("rcv")
    y, z = rcv // 8, rcv % 8
    slots = [position_of((sign(z) * (wanted - z) + 64) % 8) for wanted in range(8)]
    for half in range(2):
        for q in range(4):
            piece = response[slots[half * 4 + q]]
            rows_f32[half, q * 64 : q * 64 + 64, :] = piece.astype(jnp.float32)
        wide = jnp.concatenate(
            [rows_f32[half, pl.ds(m, 16, stride=16), :] for m in range(16)]
            + [jnp.zeros((16, 384), jnp.float32)],
            axis=1,
        )
        for shift in range(4):
            band[half, shift * 16 : shift * 16 + 16, :] = pltpu.roll(
                wide, 128 + 32 * shift, 1
            ).astype(jnp.bfloat16)
    if offset % 2:
        offset = offset * sign(lax.axis_index("shot") % 2)
    place = ((y + 4 - offset) % 4) * 2
    even_rows, odd_rows, sides = [], [], []
    for group in range(5):
        sides += [
            padded[place + half, 64 - 16 * group : 576 - 16 * group, :] for half in range(2)
        ]
        for rows, step in ((even_rows, 2 * group), (odd_rows, 2 * group + 1)):
            if step <= 8:
                for half in range(2):
                    for late in range(2):
                        first = (2 * step - late + 1) * 128
                        rows.append(band[half, :, first : first + 256])
    return jnp.concatenate(sides, axis=1), jnp.concatenate(even_rows, axis=0), jnp.concatenate(odd_rows, axis=0)


def dot(left, right):
    return jnp.dot(left, right, preferred_element_type=jnp.float32)


def add_products(offset, response, padded, band, rows, so_far, total):
    sides, even_rows, odd_rows = operands(offset, response, padded, band, rows)
    even, odd = dot(sides, even_rows), dot(sides[:, :1024], odd_rows)
    if so_far is None:
        total[:8, :] = even[:8, :]
        total[8:, :] = even[8:, :] + odd[:504, :]
    else:
        total[:8, :] = so_far[:8, :] + even[:8, :]
        total[8:, :] = so_far[8:, :] + even[8:, :] + odd[:504, :]


def first_kernel(own, padded, total, band, rows):
    add_products(0, own, padded, band, rows, None, total)


def middle_kernel(offset, response, padded, so_far, total, band, rows):
    add_products(offset, response, padded, band, rows, so_far, total)


def last_kernel(outward, padded, so_far, out, band, rows, placed):
    sides, even_rows, odd_rows = operands(1, outward, padded, band, rows)
    lane = lax.broadcasted_iota(jnp.int32, (32, 256), 1)
    carried = jnp.zeros((8, 256), jnp.float32)
    for half in range(2):
        left = sides[half * 256 : half * 256 + 256, :]
        even, odd = dot(left, even_rows), dot(left[:, :1024], odd_rows)
        shifted = jnp.concatenate([carried, odd[:248, :]], axis=0)
        carried = odd[248:, :]
        total = so_far[half * 256 : half * 256 + 256, :] + even + shifted
        turned = total.astype(jnp.bfloat16).T
        skewed = [pltpu.roll(turned[u * 32 : u * 32 + 32, :], u, 1) for u in range(8)]
        for r in range(8):
            mixed = skewed[0]
            for u in range(1, 8):
                mixed = jnp.where(lane % 8 == (r + u) % 8, skewed[u], mixed)
            mixed = pltpu.roll(mixed, (256 - r) % 256, 1)
            for part in range(2):
                lanes = mixed[:, part * 128 : part * 128 + 128].astype(jnp.float32)
                placed[half * 2 + part, pl.ds(r, 32, stride=8), :] = lanes
        for part in range(half * 2, half * 2 + 2):
            block = placed[part].reshape(32, 8, 128).astype(jnp.bfloat16)
            out[:, :, part * 128 : part * 128 + 128] = block


def call(body, shape, dtype, operands, scratch, flops=0):
    return pl.pallas_call(
        body,
        out_shape=jax.ShapeDtypeStruct(shape, dtype),
        in_specs=[VMEM] * len(operands),
        out_specs=VMEM,
        scratch_shapes=[pltpu.VMEM(s, d) for s, d in scratch],
        compiler_params=PARAMS,
        cost_estimate=pl.CostEstimate(flops=flops, bytes_accessed=2**20, transcendentals=0),
    )(*operands)


def shards(response, traces):
    f32, bf16 = jnp.float32, jnp.bfloat16
    band = [((2, 64, 19 * 128), bf16), ((2, 256, 128), f32)]

    def along_z(step):
        return lambda i: (i // 8) * 8 + step(i % 8) % 8

    def along_y(offset):
        return lambda i: (i // 8 + offset) % 4 * 8 + i % 8

    def by_core(value, way):
        pairs = []
        for i in range(lax.axis_size("shot")):
            step = along_y(way * sign(i))
            pairs += [(i * 32 + j, i * 32 + step(j)) for j in range(lax.axis_size("rcv"))]
        return lax.ppermute(value, ("shot", "rcv"), pairs)

    def along_x(i):
        return ((i // 2 + sign(i)) % 4) * 2 + i % 2

    def across_x(i):
        return (i + 4) % 8

    def swap(value):
        return spread(value, "shot", lambda i: i ^ 1)

    held = call(
        prepare_response,
        (64, 128),
        bf16,
        (response.reshape(128, 64),),
        [((128, 128), f32), ((64, 128), f32)],
    )
    held = held[None]
    both = call(
        prepare_traces,
        (2, 512, 128),
        bf16,
        (traces, swap(traces), held),
        [((2, 4, 128, 128), f32), ((2, 512, 128), f32)],
    )
    held = call(join, (2, 64, 128), bf16, (held, spread(held, "rcv", along_z(lambda z: z + sign(z)))), [], JOIN_COST)
    arrived = [
        spread(held, "rcv", along_z(lambda z, hops=hops: z - hops * sign(z))) for hops in (3, 2, 1)
    ]
    held = call(join, (8, 64, 128), bf16, (held, *arrived), [], JOIN_COST)
    across = spread(held, "rcv", along_y(2))
    outward, inward = by_core(held, 1), by_core(held, -1)

    near = spread(both, "shot", along_x)
    far = spread(both, "shot", across_x)
    pieces = (both, near, swap(near), far)
    padded = call(assemble, (8, 576, 128), bf16, pieces, [])
    work = 2 * 512 * 256 * 9 * 256
    total = call(first_kernel, (512, 256), f32, (held, padded), band, work)
    for offset, block in ((-1, inward), (2, across)):
        body = functools.partial(middle_kernel, offset)
        total = call(body, (512, 256), f32, (block, padded, total), band, work)
    return call(
        last_kernel,
        (32, 8, 512),
        bf16,
        (outward, padded, total),
        band + [((4, 256, 128), f32)],
        work,
    )


def solution(mesh):
    placed = (P("shot", "rcv", None), P("shot", "rcv", None))
    return jax.shard_map(
        shards, mesh=mesh, in_specs=placed, out_specs=P("shot", "rcv", None), check_vma=False
    )
```

```python
import functools

import jax
import jax.numpy as jnp
from jax import lax
from jax.experimental import pallas as pl
from jax.experimental.pallas import tpu as pltpu
from jax.sharding import PartitionSpec as P

RING8 = (0, 1, 5, 4, 2, 3, 7, 6)
VMEM = pl.BlockSpec(memory_space=pltpu.VMEM)
JOIN_COST = 2**33
PARAMS = pltpu.CompilerParams(vmem_limit_bytes=40 * 2**20)


def spread(value, axis, partner):
    size = lax.axis_size(axis)
    return lax.ppermute(value, axis, [(i, partner(i)) for i in range(size)])


def sign(coordinate):
    return 1 - 2 * (coordinate % 2)


def prepare_response(response, out, rows, turned):
    wide = response[...].astype(jnp.float32)
    rows[...] = jnp.concatenate([wide, jnp.zeros((128, 64), jnp.float32)], axis=1)
    by_position = jnp.concatenate([rows[pl.ds(k, 32, stride=4), :] for k in range(4)], axis=0)
    turned[...] = by_position.T[:64, :]
    skewed = [pltpu.roll(turned[pl.ds(u, 16, stride=4), :], 32 * u, 1) for u in range(4)]
    lane_block = lax.broadcasted_iota(jnp.int32, (16, 128), 1) // 32
    for k in range(4):
        mixed = skewed[0]
        for u in range(1, 4):
            mixed = jnp.where(lane_block == (k + u) % 4, skewed[u], mixed)
        out[k * 16 : k * 16 + 16, :] = pltpu.roll(mixed, (128 - 32 * k) % 128, 1).astype(jnp.bfloat16)


def prepare_traces(own, other, _, out, rows, turned):
    lane_block = lax.broadcasted_iota(jnp.int32, (64, 128), 1) // 16
    for side, traces in enumerate((own, other)):
        for part in range(4):
            lanes = traces[:, :, part * 128 : part * 128 + 128]
            rows[side, part] = lanes.astype(jnp.float32).reshape(128, 128)
        for part in range(4):
            by_receiver = [rows[side, part, pl.ds(r, 16, stride=8), :] for r in range(8)]
            turned[side, part * 128 : part * 128 + 128, :] = jnp.concatenate(by_receiver, axis=0).T
        skewed = [
            pltpu.roll(turned[side, pl.ds(d, 64, stride=8), :].astype(jnp.bfloat16), 16 * d, 1)
            for d in range(8)
        ]
        for r in range(8):
            mixed = skewed[0]
            for d in range(1, 8):
                mixed = jnp.where(lane_block == (r + d) % 8, skewed[d], mixed)
            mixed = pltpu.roll(mixed, (128 - 16 * r) % 128, 1)
            turned[side, pl.ds(r, 64, stride=8), :] = mixed.astype(jnp.float32)
        out[side] = turned[side].astype(jnp.bfloat16)


def assemble(own, near, near_swapped, far, out):
    shot = lax.axis_index("shot")
    x, core = shot // 2, shot % 2
    back = 4 - sign(core)
    blocks = (
        (own.at[0], x, core),
        (own.at[1], x, 1 - core),
        (near.at[0], x + back, core),
        (near.at[1], x + back, 1 - core),
        (near_swapped.at[0], x + 8 - back, 1 - core),
        (near_swapped.at[1], x + 8 - back, core),
        (far.at[0], x + 2, core),
        (far.at[1], x + 2, 1 - core),
    )
    for block, chip, side in blocks:
        place = (chip % 4) * 2 + side
        out[place, :64, :] = jnp.zeros((64, 128), jnp.bfloat16)
        out[place, 64:, :] = block[...]


def join(*blocks):
    out = blocks[-1]
    count = blocks[0].shape[0]
    for place, block in enumerate(blocks[:-1]):
        out[place * count : place * count + count] = block[...]


def position_of(offset):
    slot = jnp.int32(0)
    for index in range(1, 8):
        slot = jnp.where(offset == RING8[index], index, slot)
    return slot


def operands(offset, response, padded, band, rows_f32):
    rcv = lax.axis_index("rcv")
    y, z = rcv // 8, rcv % 8
    slots = [position_of((sign(z) * (wanted - z) + 64) % 8) for wanted in range(8)]
    for half in range(2):
        for q in range(4):
            piece = response[slots[half * 4 + q]]
            rows_f32[half, q * 64 : q * 64 + 64, :] = piece.astype(jnp.float32)
        wide = jnp.concatenate(
            [rows_f32[half, pl.ds(m, 16, stride=16), :] for m in range(16)]
            + [jnp.zeros((16, 384), jnp.float32)],
            axis=1,
        )
        for shift in range(4):
            band[half, shift * 16 : shift * 16 + 16, :] = pltpu.roll(
                wide, 128 + 32 * shift, 1
            ).astype(jnp.bfloat16)
    if offset % 2:
        offset = offset * sign(lax.axis_index("shot") % 2)
    place = ((y + 4 - offset) % 4) * 2
    even_rows, odd_rows, sides = [], [], []
    for group in range(5):
        sides += [
            padded[place + half, 64 - 16 * group : 576 - 16 * group, :] for half in range(2)
        ]
        for rows, step in ((even_rows, 2 * group), (odd_rows, 2 * group + 1)):
            if step <= 8:
                for half in range(2):
                    for late in range(2):
                        first = (2 * step - late + 1) * 128
                        rows.append(band[half, :, first : first + 256])
    return jnp.concatenate(sides, axis=1), jnp.concatenate(even_rows, axis=0), jnp.concatenate(odd_rows, axis=0)


def dot(left, right):
    return jnp.dot(left, right, preferred_element_type=jnp.float32)


def add_products(offset, response, padded, band, rows, so_far, total):
    sides, even_rows, odd_rows = operands(offset, response, padded, band, rows)
    even, odd = dot(sides, even_rows), dot(sides[:, :1024], odd_rows)
    if so_far is None:
        total[:8, :] = even[:8, :]
        total[8:, :] = even[8:, :] + odd[:504, :]
    else:
        total[:8, :] = so_far[:8, :] + even[:8, :]
        total[8:, :] = so_far[8:, :] + even[8:, :] + odd[:504, :]


def first_kernel(own, padded, total, band, rows):
    add_products(0, own, padded, band, rows, None, total)


def middle_kernel(offset, response, padded, so_far, total, band, rows):
    add_products(offset, response, padded, band, rows, so_far, total)


def last_kernel(second, padded, so_far, out, band, rows, placed):
    sides, even_rows, odd_rows = operands(-1, second, padded, band, rows)
    lane = lax.broadcasted_iota(jnp.int32, (32, 256), 1)
    carried = jnp.zeros((8, 256), jnp.float32)
    for half in range(2):
        left = sides[half * 256 : half * 256 + 256, :]
        even, odd = dot(left, even_rows), dot(left[:, :1024], odd_rows)
        shifted = jnp.concatenate([carried, odd[:248, :]], axis=0)
        carried = odd[248:, :]
        total = so_far[half * 256 : half * 256 + 256, :] + even + shifted
        turned = total.astype(jnp.bfloat16).T
        skewed = [pltpu.roll(turned[u * 32 : u * 32 + 32, :], u, 1) for u in range(8)]
        for r in range(8):
            mixed = skewed[0]
            for u in range(1, 8):
                mixed = jnp.where(lane % 8 == (r + u) % 8, skewed[u], mixed)
            mixed = pltpu.roll(mixed, (256 - r) % 256, 1)
            for part in range(2):
                lanes = mixed[:, part * 128 : part * 128 + 128].astype(jnp.float32)
                placed[half * 2 + part, pl.ds(r, 32, stride=8), :] = lanes
        for part in range(half * 2, half * 2 + 2):
            block = placed[part].reshape(32, 8, 128).astype(jnp.bfloat16)
            out[:, :, part * 128 : part * 128 + 128] = block


def call(body, shape, dtype, operands, scratch, flops=0):
    return pl.pallas_call(
        body,
        out_shape=jax.ShapeDtypeStruct(shape, dtype),
        in_specs=[VMEM] * len(operands),
        out_specs=VMEM,
        scratch_shapes=[pltpu.VMEM(s, d) for s, d in scratch],
        compiler_params=PARAMS,
        cost_estimate=pl.CostEstimate(flops=flops, bytes_accessed=2**20, transcendentals=0),
    )(*operands)


def shards(response, traces):
    f32, bf16 = jnp.float32, jnp.bfloat16
    band = [((2, 64, 19 * 128), bf16), ((2, 256, 128), f32)]

    def along_z(step):
        return lambda i: (i // 8) * 8 + step(i % 8) % 8

    def along_y(offset):
        return lambda i: (i // 8 + offset) % 4 * 8 + i % 8

    def by_core(value, way):
        pairs = []
        for i in range(lax.axis_size("shot")):
            step = along_y(way * sign(i))
            pairs += [(i * 32 + j, i * 32 + step(j)) for j in range(lax.axis_size("rcv"))]
        return lax.ppermute(value, ("shot", "rcv"), pairs)

    def along_x(i):
        return ((i // 2 + sign(i)) % 4) * 2 + i % 2

    def across_x(i):
        return (i + 4) % 8

    def swap(value):
        return spread(value, "shot", lambda i: i ^ 1)

    held = call(
        prepare_response,
        (64, 128),
        bf16,
        (response.reshape(128, 64),),
        [((128, 128), f32), ((64, 128), f32)],
    )
    held = held[None]
    both = call(
        prepare_traces,
        (2, 512, 128),
        bf16,
        (traces, swap(traces), held),
        [((2, 4, 128, 128), f32), ((2, 512, 128), f32)],
    )
    held = call(join, (2, 64, 128), bf16, (held, spread(held, "rcv", along_z(lambda z: z + sign(z)))), [], JOIN_COST)
    arrived = [
        spread(held, "rcv", along_z(lambda z, hops=hops: z - hops * sign(z))) for hops in (3, 2, 1)
    ]
    held = call(join, (8, 64, 128), bf16, (held, *arrived), [], JOIN_COST)
    across = spread(held, "rcv", along_y(2))
    second, first = by_core(held, -1), by_core(held, 1)

    near = spread(both, "shot", along_x)
    far = spread(both, "shot", across_x)
    pieces = (both, near, swap(near), far)
    padded = call(assemble, (8, 576, 128), bf16, pieces, [])
    work = 2 * 512 * 256 * 9 * 256
    total = call(first_kernel, (512, 256), f32, (held, padded), band, work)
    for offset, block in ((2, across), (1, first)):
        body = functools.partial(middle_kernel, offset)
        total = call(body, (512, 256), f32, (block, padded, total), band, work)
    return call(
        last_kernel,
        (32, 8, 512),
        bf16,
        (second, padded, total),
        band + [((4, 256, 128), f32)],
        work,
    )


def solution(mesh):
    placed = (P("shot", "rcv", None), P("shot", "rcv", None))
    return jax.shard_map(
        shards, mesh=mesh, in_specs=placed, out_specs=P("shot", "rcv", None), check_vma=False
    )
```
